256 devices in a mesh: lat: 16 (over x_hi, y, core), lon: 16 (over z, x_lo).
Axes of the slice: x: 4 (x_hi: 2, x_lo: 2; x = x_hi * 2 + x_lo), y: 4, z: 8, core: 2. Of those that a mesh axis runs over, the one named last changes fastest.
Arguments:
- fine_tokens: bfloat16 [384, 768, 512], P('lat', 'lon'), may hold values from -6 to 6
- merge_gain: float32 [2048], replicated, may hold values from 0.25 to 1.75
- merge_weight: bfloat16 [2048, 1024], P('lat'), may hold values from -0.125 to 0.125
- attn_gain: float32 [1024], replicated, may hold values from 0.25 to 1.75
- qkv_weight: bfloat16 [1024, 3072], P('lat'), may hold values from -0.1875 to 0.1875
- proj_weight: bfloat16 [1024, 1024], P('lat'), may hold values from -0.1875 to 0.1875
- bias_table: float32 [16, 529], replicated, may hold values from -3 to 300, as said below
- region_ids: int32 [192, 384], P('lat', 'lon'), may hold values from 0 to 3
- row_counts: int32 [16], replicated, may hold values from 1 to 12, 144 in all
- cotangent: bfloat16 [192, 384, 1024], P('lat', 'lon'), may hold values from -6 to 6
Outputs:
- output: bfloat16 [192, 384, 1024], P('lat', 'lon')
- grad_fine: bfloat16 [384, 768, 512], P('lat', 'lon')
The draws below stay inside these ranges and needn't reach their ends.
Inputs may be any that keep to these rules, and one draw needn't show every extreme that they name: row_counts[i] live rows are the first slots of latitude device i. `bias_table`: bias of each head for each relative offset.
All inputs are finite; a program needn't handle non-finite values.
Results may differ from the reference program's by a relative error of at most 0.015.
Values may be sent and summed in bfloat16 or wider, within the bound.
A program may use at most 192 MiB of HBM per device.

```python
import math
from functools import partial
import jax
import jax.numpy as jnp
import numpy as np
from jax import lax

C1 = 512
D = 1024
HEADS = 16
H2 = 12
NH2 = 192
NW2 = 384
NH1 = 384
NW1 = 768
N_LAT = 16


def draw_bias_table(key, part):
    key = jax.random.fold_in(key, 7)
    return jnp.clip(jax.random.normal(key, (HEADS, 529), jnp.float32), -3.0, 3.0)


def place_ends(values, stream_key, low, top_value):
    spot = [jax.random.randint(jax.random.fold_in(stream_key, axis), (), 0, length) for axis, length in enumerate(values.shape)]
    main_axis = values.shape.index(max(values.shape))
    beside = spot[:main_axis] + [(spot[main_axis] + 1) % values.shape[main_axis]] + spot[main_axis + 1:]
    return values.at[tuple(spot)].set(low).at[tuple(beside)].set(top_value)


def steps_of(rng, shape, cuts, low, top_value):
    def one(axis_at, parts):
        draws = jax.random.uniform(jax.random.fold_in(jax.random.fold_in(rng, 6), axis_at), (parts,), jnp.float32, low / len(cuts), top_value / len(cuts))
        return jnp.repeat(jnp.exp(draws), shape[axis_at] // parts).reshape((-1,) + (1,) * (len(shape) - axis_at - 1))

    level = one(*cuts[0])
    for cut in cuts[1:]:
        level = level * one(*cut)
    return level


def profile(number_of, total, bound, slope):
    portions = [(1 << 20) // math.isqrt(grade ** slope) + 1 for grade in range(2, number_of + 1)]
    rest, counts = total - bound - (number_of - 1), [1] * (number_of - 1)
    while rest > 0:
        free = [i for i in range(number_of - 1) if counts[i] < bound]
        mass, left = sum([portions[i] for i in free]), rest
        for i in free:
            extra = min(bound - counts[i], max(1, left * portions[i] // mass), rest)
            counts[i] = counts[i] + extra
            rest = rest - extra
    return np.array([bound] + counts)


def uneven_parts(rng, amount, total, most, lean):
    if amount == 2:
        one = jax.random.randint(rng, (), max(1, total - most), min(most, total - 1) + 1)
        return jnp.stack([one, total - one])
    lengths = jnp.asarray(profile(amount, total, most, lean), jnp.int32)
    couples = (amount - 1) // 2
    giver, receiver = lengths[1:1 + 2 * couples:2], lengths[2:2 + 2 * couples:2]
    margin = jnp.minimum(giver - 1, most - receiver)
    shifted = jax.random.randint(jax.random.fold_in(rng, 1), (couples,), 0, 1 << 20) % (margin + 1)
    lengths = lengths.at[1:1 + 2 * couples:2].set(giver - shifted).at[2:2 + 2 * couples:2].set(receiver + shifted)
    return lengths[jax.random.permutation(jax.random.fold_in(rng, 2), amount)]


def bell_draw(rng, shape, spread, limit, cuts=(), held_as=jnp.bfloat16):
    entries = jax.random.normal(rng, shape, jnp.float32) * spread
    if len(cuts) > 0:
        entries = steps_of(rng, shape, cuts, -0.22, 0.18) * entries
    return jnp.clip(entries, min=-limit, max=limit).astype(held_as)


def setup_inputs(seed: int = 0) -> dict:
    key_of = jax.random.split(jax.random.key(seed), 11)
    return {
        "fine_tokens": bell_draw(key_of[0], (NH1, NW1, C1), 1.0, 6.0, ((0, 16), (1, 16))),
        "merge_gain": jnp.clip(1.0 + 0.15 * jax.random.normal(key_of[1], (4 * C1,), jnp.float32), 0.25, 1.75),
        "merge_weight": bell_draw(key_of[2], (4 * C1, D), (4 * C1) ** -0.5, 0.125, ((0, 16),)),
        "attn_gain": jnp.clip(1.0 + 0.15 * jax.random.normal(key_of[3], (D,), jnp.float32), 0.25, 1.75),
        "qkv_weight": bell_draw(key_of[4], (D, 3 * D), D ** -0.5, 0.1875, ((0, 16),)),
        "proj_weight": bell_draw(key_of[5], (D, D), D ** -0.5, 0.1875, ((0, 16),)),
        "bias_table": draw_bias_table(jax.random.fold_in(key_of[10], 71), 0),
        "region_ids": place_ends(jax.random.randint(key_of[7], (NH2, NW2), 0, 4), jax.random.fold_in(key_of[7], 1), 0, 3).astype(jnp.int32),
        "row_counts": uneven_parts(key_of[8], N_LAT, N_LAT * H2 * 3 // 4, H2, 0).astype(jnp.int32),
        "cotangent": bell_draw(key_of[9], (NH2, NW2, D), 1.0, 6.0, ((0, 16), (1, 16))),
    }


NORM_EPS = 1e-05
MASKED = -1000000000.0

def offset_table():
    position = np.arange(144)
    win_row = position // 12
    win_col = position % 12
    return (win_row[:, None] - win_row[None, :] + 11) * 23 + (win_col[:, None] - win_col[None, :] + 11)

def norm_rows(values):
    average = lax.optimization_barrier(jnp.mean(values, axis=-1, keepdims=True))
    centred = values - average
    inv_scale = lax.rsqrt(lax.optimization_barrier(jnp.mean(centred * centred, axis=-1, keepdims=True)) + NORM_EPS)
    return (centred * inv_scale, inv_scale)

def norm_back(values, gain, upstream):
    normed, inv_scale = norm_rows(values)
    weighted = upstream * gain
    first_term = lax.optimization_barrier(jnp.mean(weighted, axis=-1, keepdims=True))
    second_term = lax.optimization_barrier(jnp.mean(weighted * normed, axis=-1, keepdims=True))
    return inv_scale * (weighted - first_term - normed * second_term)

def merge_patches(values):
    half_rows = values.shape[0] // 2
    half_cols = values.shape[1] // 2
    channels = values.shape[2]
    return values.reshape(half_rows, 2, half_cols, 2, channels).transpose(0, 2, 3, 1, 4).reshape(half_rows, half_cols, 4 * channels)

def split_patches(values):
    half_rows, half_cols, merged_width = values.shape
    channels = merged_width // 4
    return values.reshape(half_rows, half_cols, 2, 2, channels).transpose(0, 3, 1, 2, 4).reshape(2 * half_rows, 2 * half_cols, channels)

def to_windows(values):
    win_rows = values.shape[0] // 12
    win_cols = values.shape[1] // 12
    trailing = values.shape[2:]
    tiled = jnp.moveaxis(values.reshape((win_rows, 12, win_cols, 12) + trailing), 2, 1)
    return tiled.reshape((win_rows * win_cols, 144) + trailing)

def from_windows(values, win_rows, win_cols):
    trailing = values.shape[2:]
    tiled = jnp.moveaxis(values.reshape((win_rows, win_cols, 12, 12) + trailing), 1, 2)
    return tiled.reshape((win_rows * 12, win_cols * 12) + trailing)

def rounded(values):
    return lax.optimization_barrier(values.astype(jnp.bfloat16)).astype(jnp.float32)

def window_pass(pieces, offsets, head_count):
    queries, keys, values, query_tag, key_tag, upstream = pieces
    model_width = queries.shape[1]
    head_dim = model_width // head_count
    factor = head_dim ** (-0.5)
    query_heads = queries.astype(jnp.float32).reshape(144, head_count, head_dim)
    key_heads = keys.astype(jnp.float32).reshape(144, head_count, head_dim)
    value_heads = values.astype(jnp.float32).reshape(144, head_count, head_dim)
    scores = jnp.einsum('qhd,khd->hqk', query_heads, key_heads) * factor + offsets
    allowed = (query_tag[:, None] == key_tag[None, :]) & (key_tag[None, :] > 0)
    scores = jnp.where(allowed[None], scores, MASKED)
    highest = lax.optimization_barrier(jnp.max(scores, axis=-1, keepdims=True))
    powers = jnp.exp(scores - highest)
    weights = powers / lax.optimization_barrier(jnp.sum(powers, axis=-1, keepdims=True))
    weights_round = rounded(weights)
    alive = (query_tag > 0).astype(jnp.float32)
    attended = (jnp.einsum('hqk,khd->qhd', weights_round, value_heads) * alive[:, None, None]).astype(jnp.bfloat16)
    grad_heads = upstream.astype(jnp.float32).reshape(144, head_count, head_dim)
    row_dots = lax.optimization_barrier(jnp.sum(grad_heads * attended.astype(jnp.float32), axis=-1))
    grad_scores = jnp.einsum('qhd,khd->hqk', grad_heads, value_heads)
    grad_logits = rounded(weights * (grad_scores - jnp.transpose(row_dots)[:, :, None]))
    grad_query = (jnp.einsum('hqk,khd->qhd', grad_logits, key_heads) * factor).astype(jnp.bfloat16)
    grad_key = (jnp.einsum('hqk,qhd->khd', grad_logits, query_heads) * factor).astype(jnp.bfloat16)
    grad_value = jnp.einsum('hqk,qhd->khd', weights_round, grad_heads).astype(jnp.bfloat16)
    return tuple((member.reshape(144, model_width) for member in (attended, grad_query, grad_key, grad_value)))

def arrange(values):
    padded = jnp.pad(values, ((6, 6),) + ((0, 0),) * (values.ndim - 1))
    return to_windows(jnp.roll(padded, 6, axis=1))

def restore(values, grid_rows, grid_cols):
    tiled = from_windows(values, grid_rows // 12 + 1, grid_cols // 12)
    return jnp.roll(tiled, -6, axis=1)[6:6 + grid_rows]

def reference(fine_tokens, merge_gain, merge_weight, attn_gain, qkv_weight, proj_weight, bias_table, region_ids, row_counts, cotangent):
    grid_rows, grid_cols = region_ids.shape
    model_width = proj_weight.shape[0]
    head_count = bias_table.shape[0]
    token_count = grid_rows * grid_cols
    patches = merge_patches(fine_tokens.astype(jnp.float32)).reshape(token_count, -1)
    patch_normed = (norm_rows(patches)[0] * merge_gain).astype(jnp.bfloat16)
    merged = jnp.dot(patch_normed, merge_weight, preferred_element_type=jnp.float32).astype(jnp.bfloat16)
    merged_wide = merged.astype(jnp.float32)
    normed = (norm_rows(merged_wide)[0] * attn_gain).astype(jnp.bfloat16)
    projected = jnp.dot(normed, qkv_weight, preferred_element_type=jnp.float32).astype(jnp.bfloat16)
    projected = projected.reshape(grid_rows, grid_cols, 3 * model_width)
    row_index = jnp.arange(grid_rows, dtype=jnp.int32)
    alive_rows = row_index % H2 < row_counts[row_index // H2]
    region_tag = (region_ids + 1) * alive_rows.astype(jnp.int32)[:, None]
    upstream = jnp.dot(cotangent.reshape(token_count, model_width), proj_weight.T, preferred_element_type=jnp.float32)
    upstream = (upstream.reshape(grid_rows, grid_cols, model_width) * alive_rows.astype(jnp.float32)[:, None, None]).astype(jnp.bfloat16)
    offsets = bias_table[:, offset_table()]
    windows = (arrange(projected[..., :model_width]), arrange(projected[..., model_width:2 * model_width]), arrange(projected[..., 2 * model_width:]), arrange(region_tag), arrange(region_tag), arrange(upstream))
    results = lax.map(partial(window_pass, offsets=offsets, head_count=head_count), windows)
    attended, grad_query, grad_key, grad_value = [restore(member, grid_rows, grid_cols) for member in results]
    output = merged_wide + jnp.dot(attended.reshape(token_count, model_width), proj_weight, preferred_element_type=jnp.float32)
    output = output.astype(jnp.bfloat16).reshape(grid_rows, grid_cols, model_width)
    grad_proj = jnp.concatenate([grad_query, grad_key, grad_value], axis=-1).reshape(token_count, 3 * model_width)
    grad_normed = jnp.dot(grad_proj, qkv_weight.T, preferred_element_type=jnp.float32)
    grad_merged = cotangent.reshape(token_count, model_width).astype(jnp.float32) + norm_back(merged_wide, attn_gain, grad_normed)
    grad_patches = jnp.dot(grad_merged.astype(jnp.bfloat16), merge_weight.T, preferred_element_type=jnp.float32)
    grad_fine = split_patches(norm_back(patches, merge_gain, grad_patches).reshape(grid_rows, grid_cols, -1)).astype(jnp.bfloat16)
    return (output, grad_fine)
```

```python
import functools

import jax
import jax.numpy as jnp
from jax import lax
from jax.experimental import pallas as pl
from jax.experimental.pallas import tpu as pltpu
from jax.sharding import PartitionSpec as P

MESH = pl.DeviceIdType.MESH
BF16 = jnp.bfloat16
F32 = jnp.float32
NORM_EPS = 1e-05
MASKED = -1000000000.0
NT = (((1,), (1,)), ((), ()))
TN = (((0,), (0,)), ((), ()))

KEYS = [(1, 0), (0, 3), (0, 1), (0, 2), (1, 3), (1, 1), (1, 2)]
CROSS = [(1, 0), (0, 3), (0, 1), (0, 2, 0), (0, 2, 1), (1, 3), (1, 1), (1, 2)]
RID = {("c",) + k: i for i, k in enumerate(CROSS)}
RID.update({("r",) + k: 8 + i for i, k in enumerate(KEYS)})
RID.update({("k",) + k: 15 + i for i, k in enumerate(KEYS)})
RID.update({("q",) + k: 22 + i for i, k in enumerate(KEYS)})
RID[("own",)] = 29
N_IDS = 30
LINK = {
    (1, 0): "zp",
    (0, 3): "zm",
    (0, 1): "xl",
    (0, 2): "zp",
    (1, 3): "xl",
    (1, 1): "zm",
    (1, 2): "zp",
}

TC, TL, BR, BL, BLX = 0, 1, 2, 3, 4
SLOT = ((0, 80), (80, 48), (128, 48), (176, 48), (224, 48))
IN_ROWS, OUT_ROWS = 272, 224


class Gather:
    def __init__(self, shards, fulls, send_sem, recv_sem, local_sem):
        self.shards, self.fulls = shards, fulls
        self.send_sem, self.recv_sem, self.local_sem = send_sem, recv_sem, local_sem
        lat, lon = lax.axis_index("lat"), lax.axis_index("lon")
        a, y, k = lat // 8, (lat // 2) % 4, lat % 2
        z, xlo = lon // 2, lon % 2
        self.a, self.y, self.k = a, y, k
        self.c = (xlo + a + z) % 2

        def at(a_, y_, k_):
            return a_ * 8 + y_ * 2 + k_

        self.near = dict(
            yp=(at(a, (y + 1) % 4, k), lon),
            ym=(at(a, (y + 3) % 4, k), lon),
            xh=(at(1 - a, y, k), z * 2 + (1 - xlo)),
            xl=(lat, z * 2 + (1 - xlo)),
            zp=(lat, ((z + 1) % 8) * 2 + xlo),
            zm=(lat, ((z + 7) % 8) * 2 + xlo),
            core=(at(a, y, 1 - k), lon),
        )
        self.sent, self.local = [], []
        self.count = [0] * len(shards)

    def rows(self, w, key, half, core):
        r = self.shards[w].shape[0]
        a = self.a if key[0] == 0 else 1 - self.a
        s = a * 8 + ((self.y + key[1]) % 4) * 2 + core
        if half is None:
            return pl.ds(pl.multiple_of(s * r, r), r)
        off, n = half * (r // 2), r // 2
        if len(key) == 3:
            off, n = off + key[2] * (r // 4), r // 4
        return pl.ds(pl.multiple_of(s * r + off, n), n)

    def copy(self, w, rid, src, dst, dev, i):
        return pltpu.make_async_remote_copy(
            src_ref=src,
            dst_ref=dst,
            send_sem=self.send_sem.at[w, i],
            recv_sem=self.recv_sem.at[w, RID[rid]],
            device_id=dev,
            device_id_type=MESH,
        )

    def send(self, w, where, to, rid, src=None):
        full = self.fulls[w]
        i = self.count[w]
        self.count[w] += 1
        src = full.at[where] if src is None else src
        cp = self.copy(w, rid, src, full.at[where], self.near[to], i)
        cp.start()
        self.sent.append(cp)

    def recv(self, w, rid, where):
        part = self.fulls[w].at[where]
        self.copy(w, rid, part, part, self.near["core"], 0).wait_recv()

    def s0(self, w):
        shard = self.shards[w]
        r = shard.shape[0]
        where = self.rows(w, (0, 0), self.c, self.k)
        half = shard.at[pl.ds(pl.multiple_of(self.c * (r // 2), r // 2), r // 2)]
        self.send(w, where, "xh", ("c", 1, 0), half)
        self.send(w, where, "yp", ("c", 0, 3), half)
        self.send(w, where, "ym", ("c", 0, 1), half)
        whole = self.rows(w, (0, 0), None, self.k)
        self.send(w, whole, "core", ("own",), shard)
        cp = pltpu.make_async_copy(shard, self.fulls[w].at[whole], self.local_sem.at[w])
        cp.start()
        self.local.append(cp)

    def spread(self, w, key):
        where = self.rows(w, key, self.c, self.k)
        self.send(w, where, LINK[key], ("r",) + key)
        self.send(w, where, "core", ("k",) + key)

    def s1(self, w):
        c, k = self.c, self.k
        where = self.rows(w, (1, 0), c, k)
        self.recv(w, ("c", 1, 0), where)
        self.send(w, where, "yp", ("c", 1, 3))
        self.send(w, where, "ym", ("c", 1, 1))
        self.spread(w, (1, 0))
        self.recv(w, ("c", 0, 3), self.rows(w, (0, 3), c, k))
        self.send(w, self.rows(w, (0, 3, 0), c, k), "yp", ("c", 0, 2, 0))
        self.spread(w, (0, 3))
        self.recv(w, ("c", 0, 1), self.rows(w, (0, 1), c, k))
        self.send(w, self.rows(w, (0, 1, 1), c, k), "ym", ("c", 0, 2, 1))
        self.spread(w, (0, 1))

    def s2(self, w):
        c, k = self.c, self.k
        self.recv(w, ("c", 0, 2, 0), self.rows(w, (0, 2, 0), c, k))
        self.recv(w, ("c", 0, 2, 1), self.rows(w, (0, 2, 1), c, k))
        self.send(w, self.rows(w, (0, 2), c, k), "xh", ("c", 1, 2))
        self.spread(w, (0, 2))

    def s3(self, w):
        for key in ((1, 3), (1, 1), (1, 2)):
            self.recv(w, ("c",) + key, self.rows(w, key, self.c, self.k))
            self.spread(w, key)

    def s4(self, w):
        for key in KEYS:
            where = self.rows(w, key, 1 - self.c, self.k)
            self.recv(w, ("r",) + key, where)
            self.send(w, where, "core", ("q",) + key)

    def fin(self, w):
        self.recv(w, ("own",), self.rows(w, (0, 0), None, 1 - self.k))
        for key in KEYS:
            self.recv(w, ("k",) + key, self.rows(w, key, self.c, 1 - self.k))
            self.recv(w, ("q",) + key, self.rows(w, key, 1 - self.c, 1 - self.k))
        self.local[w].wait()

    def drain(self):
        for cp in self.sent:
            cp.wait_send()


def over12(v):
    return (v * 171) >> 11


def over6(v):
    return (v * 171) >> 10


def window_source(d, lat):
    second = d >= 144
    e = jnp.where(second, d - 144, d)
    r = over12(e)
    c = e - 12 * r
    none = jnp.full(d.shape, -1, jnp.int32)
    lats = jnp.zeros(d.shape, jnp.int32) + lat
    upper = r < 6
    left = c < 6
    edge = (r - 6) * 6 + (c - 6)
    last = lats == 15
    first = lats == 0
    own_a = jnp.where(upper, (6 + r) * 24 + 6 + c, jnp.where(last & left, r * 24 + 18 + c, none))
    in_a = jnp.where(
        upper,
        none,
        jnp.where(last, jnp.where(left, none, SLOT[BLX][0] + edge), (r - 6) * 12 + c),
    )
    own_b = jnp.where(
        upper,
        jnp.where(first, r * 24 + 6 + c, none),
        jnp.where(left, (r - 6) * 24 + 18 + c, none),
    )
    in_top = jnp.where(left, SLOT[BR][0] + r * 6 + c, SLOT[BL][0] + r * 6 + c - 6)
    in_b = jnp.where(
        upper,
        jnp.where(first, none, in_top),
        jnp.where(left, none, SLOT[TL][0] + edge),
    )
    return jnp.where(second, own_b, own_a), jnp.where(second, in_b, in_a)


def slot_source(s):
    none = jnp.full(s.shape, -1, jnp.int32)
    r12 = over12(s)
    tc = jnp.where(s < 72, r12 * 24 + 6 + s - 12 * r12, none)

    def corner(base, row, col):
        t = s - base
        r = over6(t)
        return jnp.where(t < 36, (row + r) * 24 + col + t - 6 * r, none)

    tl, br, bl = corner(80, 0, 0), corner(128, 6, 18), corner(176, 6, 0)
    return jnp.where(s < 80, tc, jnp.where(s < 128, tl, jnp.where(s < 176, br, bl)))


def column(n):
    return lax.broadcasted_iota(jnp.int32, (n, 1), 0)


def line(n):
    return lax.broadcasted_iota(jnp.int32, (1, n), 1)


def pick(source, rows, cols):
    axis = 1 if source.shape[1] == 1 else 0
    place = lax.broadcasted_iota(jnp.int32, (rows, cols), axis)
    return (source == place).astype(F32).astype(BF16)


def dot(a, b):
    return jnp.dot(a, b, preferred_element_type=F32)


def dot_nt(a, b):
    return lax.dot_general(a, b, NT, preferred_element_type=F32)


def dot_tn(a, b):
    return lax.dot_general(a, b, TN, preferred_element_type=F32)


def norm_rows(v):
    n = v.shape[-1]
    centred = v - jnp.sum(v, axis=-1, keepdims=True) * (1.0 / n)
    inv = lax.rsqrt(jnp.sum(centred * centred, axis=-1, keepdims=True) * (1.0 / n) + NORM_EPS)
    return centred * inv, inv


def kernel(
    fine,
    merge_gain,
    merge_shard,
    attn_gain,
    qkv_shard,
    proj_shard,
    table,
    region,
    counts,
    cot,
    out,
    grad_fine,
    merge,
    qkv_w,
    proj,
    g_send,
    g_recv,
    g_local,
    f_send,
    f_recv,
    b_send,
    b_recv,
    out_cot,
    out_mer,
    in_cot,
    in_mer,
    back_out,
    back_grad,
    home_out,
    home_grad,
    patch_n,
    merged_home,
    win_mer,
    win_cot,
    normed,
    proj_all,
    upstream,
    attended,
    grad_all,
    wide,
    grad_patch,
    lines,
    split,
    bias,
    mask,
    tag_pad,
):
    lat, lon = lax.axis_index("lat"), lax.axis_index("lon")
    up = ((lat + 15) % 16, lon)
    down = ((lat + 1) % 16, lon)
    left = (lat, (lon + 15) % 16)
    right = (lat, (lon + 1) % 16)
    down_left = ((lat + 1) % 16, (lon + 15) % 16)
    up_right = ((lat + 15) % 16, (lon + 1) % 16)
    gather = Gather((merge_shard, qkv_shard, proj_shard), (merge, qkv_w, proj), g_send, g_recv, g_local)

    for ref in (in_cot, in_mer, home_out, home_grad):
        ref[...] = jnp.zeros_like(ref)
    barrier = pltpu.get_barrier_semaphore()
    partners = list(gather.near.values()) + [up, down, left, right, down_left, up_right]
    for dev in partners:
        pl.semaphore_signal(barrier, inc=1, device_id=dev, device_id_type=MESH)
    pl.semaphore_wait(barrier, len(partners))

    not_first, not_last, is_last = lat > 0, lat < 15, lat == 15

    def forward(m, src, dst, do):
        def go(slot_from, slot_to, dev):
            f0, n = SLOT[slot_from]
            t0 = SLOT[slot_to][0]
            do(
                pltpu.make_async_remote_copy(
                    src_ref=src.at[pl.ds(f0, n)],
                    dst_ref=dst.at[pl.ds(t0, n)],
                    send_sem=f_send.at[m, slot_from],
                    recv_sem=f_recv.at[m, slot_to],
                    device_id=dev,
                    device_id_type=MESH,
                )
            )

        go(TL, TL, left)

        @pl.when(not_first)
        def _():
            go(TC, TC, up)

        @pl.when(not_last)
        def _():
            go(BR, BR, down)
            go(BL, BL, down_left)

        @pl.when(is_last)
        def _():
            go(BL, BLX, left)

    def forward_recv(m, dst):
        def got(slot):
            f0, n = SLOT[slot]
            part = dst.at[pl.ds(f0, n)]
            pltpu.make_async_remote_copy(
                src_ref=part,
                dst_ref=part,
                send_sem=f_send.at[m, 0],
                recv_sem=f_recv.at[m, slot],
                device_id=right,
                device_id_type=MESH,
            ).wait_recv()

        got(TL)

        @pl.when(not_last)
        def _():
            got(TC)

        @pl.when(not_first)
        def _():
            got(BR)
            got(BL)

        @pl.when(is_last)
        def _():
            got(BLX)

    def backward(m, src, dst, do):
        def go(slot_from, slot_to, dev):
            f0, n = SLOT[slot_from]
            t0 = SLOT[slot_to][0]
            do(
                pltpu.make_async_remote_copy(
                    src_ref=src.at[pl.ds(f0, n)],
                    dst_ref=dst.at[pl.ds(t0, n)],
                    send_sem=b_send.at[m, slot_from],
                    recv_sem=b_recv.at[m, slot_to],
                    device_id=dev,
                    device_id_type=MESH,
                )
            )

        go(TL, TL, right)

        @pl.when(not_last)
        def _():
            go(TC, TC, down)

        @pl.when(not_first)
        def _():
            go(BR, BR, up)
            go(BL, BL, up_right)

        @pl.when(is_last)
        def _():
            go(BLX, BL, right)

    def backward_recv(m, dst):
        def got(slot):
            f0, n = SLOT[slot]
            part = dst.at[pl.ds(f0, n)]
            pltpu.make_async_remote_copy(
                src_ref=part,
                dst_ref=part,
                send_sem=b_send.at[m, 0],
                recv_sem=b_recv.at[m, slot],
                device_id=right,
                device_id_type=MESH,
            ).wait_recv()

        got(TL)
        got(BL)

        @pl.when(not_first)
        def _():
            got(TC)

        @pl.when(not_last)
        def _():
            got(BR)

    def start(cp):
        cp.start()

    def sent(cp):
        cp.wait_send()

    gather.s0(0)
    tag_pad[...] = jnp.zeros_like(tag_pad)
    tag_pad[0:12, 0:24] = (region[...] + 1).astype(F32)
    cell = column(288)
    cell_row = (cell * 171) >> 12
    cell_col = cell - 24 * cell_row
    row_pick = (cell_row == lax.broadcasted_iota(jnp.int32, (288, 16), 1)).astype(F32).astype(BF16)
    tags = dot(row_pick, tag_pad[...].astype(BF16))
    lanes128 = lax.broadcasted_iota(jnp.int32, (288, 128), 1)
    tag = jnp.sum(jnp.where(lanes128 == cell_col, tags, 0.0), axis=-1, keepdims=True)
    tag = tag * (cell_row < counts[lat]).astype(F32)
    tag_home = jnp.broadcast_to(tag, (288, 128)).astype(BF16)
    to_slots = pick(slot_source(column(OUT_ROWS)), OUT_ROWS, 288)
    out_cot[:, 0:1024] = dot(to_slots, cot[...]).astype(BF16)
    out_cot[:, 1024:1152] = dot(to_slots, tag_home).astype(BF16)
    forward(0, out_cot, in_cot, start)

    o = column(192)
    block = jnp.where(o < 48, 0, jnp.where(o < 96, 1, jnp.where(o < 144, 2, 3)))
    within = o - 48 * block
    wr = (within >= 24).astype(jnp.int32)
    wc = within - 24 * wr
    to_blocks = pick((2 * wr + (block & 1)) * 48 + 2 * wc + (block >> 1), 192, 192)

    def patch_stats(g):
        raw = dot(to_blocks, fine[pl.ds(pl.multiple_of(g * 192, 192), 192), :])
        parts = [raw[48 * b : 48 * b + 48] for b in range(4)]
        average = sum(jnp.sum(p, axis=-1, keepdims=True) for p in parts) * (1.0 / 2048)
        parts = [p - average for p in parts]
        spread = sum(jnp.sum(p * p, axis=-1, keepdims=True) for p in parts) * (1.0 / 2048)
        inv = lax.rsqrt(spread + NORM_EPS)
        return [p * inv for p in parts], inv

    def patches(g, _):
        parts, _inv = patch_stats(g)
        at = pl.ds(pl.multiple_of(g * 48, 48), 48)
        for b in range(4):
            gain = merge_gain[:, 512 * b : 512 * b + 512]
            patch_n[at, 512 * b : 512 * b + 512] = (parts[b] * gain).astype(BF16)
        return 0

    def bias_lines(c, _):
        lane = line(384)
        u = over12(lane)
        index = jnp.where(lane < 276, u * 23 + (lane - 12 * u) - c + 11, -1)
        three = dot(split[...], pick(index, 640, 384))
        lines[c] = three[0:16] + three[16:32] + three[32:48]
        return 0

    gather.s1(0)
    gather.s0(1)
    lax.fori_loop(0, 3, patches, 0)
    gather.s2(0)
    lax.fori_loop(3, 6, patches, 0)
    gather.s3(0)
    gather.s1(1)
    gather.s0(2)
    t = table[...]
    high = t.astype(BF16)
    rest = t - high.astype(F32)
    middle = rest.astype(BF16)
    split[...] = jnp.zeros_like(split)
    split[0:16, 0:529] = high
    split[16:32, 0:529] = middle
    split[32:48, 0:529] = (rest - middle.astype(F32)).astype(BF16)
    lax.fori_loop(0, 6, bias_lines, 0)
    gather.s4(0)
    gather.s2(1)
    lax.fori_loop(6, 12, bias_lines, 0)
    gather.fin(0)

    def merge_tile(n, _):
        at = pl.ds(pl.multiple_of(n * 256, 256), 256)
        merged_home[:, at] = dot(patch_n[...], merge[:, at]).astype(BF16)
        return 0

    lax.fori_loop(0, 4, merge_tile, 0)
    out_mer[...] = dot(to_slots, merged_home[...]).astype(BF16)
    forward(1, out_mer, in_mer, start)

    gather.s3(1)
    gather.s1(2)
    for h in range(16):
        some = lines[:, h, :]
        for r in range(12):
            bias[h, 12 * r : 12 * r + 12, :] = some[:, 12 * (11 - r) : 12 * (11 - r) + 144]
    gather.s4(1)
    gather.s2(2)

    own, came = window_source(column(288), lat)
    from_home = pick(own, 288, 288)
    from_slots = pick(came, 288, IN_ROWS)
    forward_recv(0, in_cot)
    win_cot[...] = (dot(from_home, cot[...]) + dot(from_slots, in_cot[:, 0:1024])).astype(BF16)
    win_tag = dot(from_home, tag_home) + dot(from_slots, in_cot[:, 1024:1152])
    d = lax.broadcasted_iota(jnp.int32, (288, 128), 0)
    apart = ((lat == 15) & (d >= 72) & (d < 144)) | ((lat == 0) & (d >= 144) & (d < 216))
    live = (win_tag > 0).astype(F32)
    win_tag = win_tag + 8.0 * live * apart.astype(F32)
    for w in range(2):
        at = slice(144 * w, 144 * w + 144)
        key_tag = win_tag[at, 0:1]
        query_tag = jnp.transpose(win_tag[at])[0:1]
        allowed = (key_tag == query_tag) & (key_tag > 0)
        mask[w] = jnp.where(allowed, 0.0, MASKED)
    gather.s3(2)
    gather.s4(2)
    forward_recv(1, in_mer)
    win_mer[...] = (dot(from_home, merged_home[...]) + dot(from_slots, in_mer[...])).astype(BF16)

    def norm_chunk(g, _):
        at = pl.ds(pl.multiple_of(g * 48, 48), 48)
        normed[at, :] = (norm_rows(win_mer[at, :].astype(F32))[0] * attn_gain[...]).astype(BF16)
        return 0

    lax.fori_loop(0, 6, norm_chunk, 0)
    gather.fin(1)

    def qkv_tile(n, _):
        at = pl.ds(pl.multiple_of(n * 256, 256), 256)
        proj_all[:, at] = dot(normed[...], qkv_w[:, at]).astype(BF16)
        return 0

    lax.fori_loop(0, 12, qkv_tile, 0)
    gather.fin(2)
    live_col = live[:, 0:1]

    def upstream_tile(n, _):
        at = pl.ds(pl.multiple_of(n * 256, 256), 256)
        upstream[:, at] = (dot_nt(win_cot[...], proj[at, :]) * live_col).astype(BF16)
        return 0

    lax.fori_loop(0, 4, upstream_tile, 0)

    lane = lax.broadcasted_iota(jnp.int32, (144, 128), 1)

    def attend(pair, _):
        off = pl.multiple_of(pair * 128, 128)
        for w in range(2):
            rows = pl.ds(144 * w, 144)
            q = proj_all[rows, pl.ds(off, 128)] * jnp.asarray(0.125, BF16)
            k = proj_all[rows, pl.ds(1024 + off, 128)]
            v = proj_all[rows, pl.ds(2048 + off, 128)]
            u = upstream[rows, pl.ds(off, 128)]
            sums = [0.0, 0.0, 0.0, 0.0]
            for e in range(2):
                half = (lane < 64) if e == 0 else (lane >= 64)
                qe, ke, ve, ue = [jnp.where(half, x, jnp.zeros_like(x)) for x in (q, k, v, u)]
                scores = dot_nt(ke, q) + bias[2 * pair + e] + mask[w]
                powers = jnp.exp(scores - jnp.max(scores, axis=0, keepdims=True))
                probs = powers * (1.0 / jnp.sum(powers, axis=0, keepdims=True))
                low = probs.astype(BF16)
                grads = dot_nt(ve, u)
                rows_dot = jnp.sum(probs * grads, axis=0, keepdims=True)
                logits = (probs * (grads - rows_dot)).astype(BF16)
                terms = (dot_tn(low, ve), dot_tn(logits, ke), dot(logits, qe), dot(low, ue))
                sums = [s + x for s, x in zip(sums, terms)]
            alive = live[144 * w : 144 * w + 144]
            attended[rows, pl.ds(off, 128)] = (sums[0] * alive).astype(BF16)
            grad_all[rows, pl.ds(off, 128)] = (sums[1] * 0.125).astype(BF16)
            grad_all[rows, pl.ds(1024 + off, 128)] = sums[2].astype(BF16)
            grad_all[rows, pl.ds(2048 + off, 128)] = sums[3].astype(BF16)
        return 0

    lax.fori_loop(0, 8, attend, 0)

    def out_tile(n, _):
        at = pl.ds(pl.multiple_of(n * 256, 256), 256)
        total = win_mer[:, at].astype(F32) + dot(attended[...], proj[:, at])
        normed[:, at] = total.astype(BF16)
        return 0

    lax.fori_loop(0, 4, out_tile, 0)
    own_l, came_l = window_source(line(288), lat)
    to_in_slots = pick(came_l, IN_ROWS, 288)
    to_home = pick(own_l, 288, 288)
    slots_home = pick(slot_source(line(OUT_ROWS)), 288, OUT_ROWS)
    back_out[...] = dot(to_in_slots, normed[...]).astype(BF16)
    backward(0, back_out, home_out, start)

    def grad_tile(n, _):
        at = pl.ds(pl.multiple_of(n * 256, 256), 256)
        wide[:, at] = dot_nt(grad_all[...], qkv_w[at, :])
        return 0

    lax.fori_loop(0, 4, grad_tile, 0)

    def norm_back_chunk(g, _):
        at = pl.ds(pl.multiple_of(g * 48, 48), 48)
        n, inv = norm_rows(win_mer[at, :].astype(F32))
        weighted = wide[at, :] * attn_gain[...]
        first = jnp.sum(weighted, axis=-1, keepdims=True) * (1.0 / 1024)
        second = jnp.sum(weighted * n, axis=-1, keepdims=True) * (1.0 / 1024)
        back = win_cot[at, :].astype(F32) + inv * (weighted - first - n * second)
        win_cot[at, :] = back.astype(BF16)
        return 0

    lax.fori_loop(0, 6, norm_back_chunk, 0)
    back_grad[...] = dot(to_in_slots, win_cot[...]).astype(BF16)
    backward(1, back_grad, home_grad, start)
    backward_recv(0, home_out)
    out[...] = (dot(to_home, normed[...]) + dot(slots_home, home_out[...])).astype(BF16)
    backward_recv(1, home_grad)
    merged_home[...] = (dot(to_home, win_cot[...]) + dot(slots_home, home_grad[...])).astype(BF16)

    def patch_tile(n, _):
        at = pl.ds(pl.multiple_of(n * 256, 256), 256)
        grad_patch[:, at] = dot_nt(merged_home[...], merge[at, :])
        return 0

    lax.fori_loop(0, 8, patch_tile, 0)

    def patch_back(g, _):
        parts, inv = patch_stats(g)
        at = pl.ds(pl.multiple_of(g * 48, 48), 48)
        weighted = [
            grad_patch[at, 512 * b : 512 * b + 512] * merge_gain[:, 512 * b : 512 * b + 512]
            for b in range(4)
        ]
        first = sum(jnp.sum(x, axis=-1, keepdims=True) for x in weighted) * (1.0 / 2048)
        second = sum(
            jnp.sum(x * n, axis=-1, keepdims=True) for x, n in zip(weighted, parts)
        ) * (1.0 / 2048)
        back = [(inv * (x - first - n * second)).astype(BF16) for x, n in zip(weighted, parts)]
        tokens = dot_tn(to_blocks, jnp.concatenate(back, axis=0))
        grad_fine[pl.ds(pl.multiple_of(g * 192, 192), 192), :] = tokens.astype(BF16)
        return 0

    lax.fori_loop(0, 6, patch_back, 0)

    gather.drain()
    forward(0, out_cot, in_cot, sent)
    forward(1, out_mer, in_mer, sent)
    backward(0, back_out, home_out, sent)
    backward(1, back_grad, home_grad, sent)


def local(fine, merge_gain, merge_w, attn_gain, qkv_w, proj_w, table, region, counts, cot):
    whole = pl.BlockSpec(memory_space=pltpu.VMEM)
    away = pl.BlockSpec(memory_space=pl.ANY)
    smem = pl.BlockSpec(memory_space=pltpu.SMEM)
    dma = pltpu.SemaphoreType.DMA

    def held(*shape, dtype=BF16):
        return pltpu.VMEM(shape, dtype)

    out, grad_fine = pl.pallas_call(
        kernel,
        out_shape=[
            jax.ShapeDtypeStruct((288, 1024), BF16),
            jax.ShapeDtypeStruct((1152, 512), BF16),
        ],
        in_specs=[whole, whole, away, whole, away, away, whole, whole, smem, whole],
        out_specs=[whole, whole],
        scratch_shapes=[
            held(2048, 1024),
            held(1024, 3072),
            held(1024, 1024),
            dma((3, N_IDS)),
            dma((3, N_IDS)),
            dma((3,)),
            dma((2, 5)),
            dma((2, 5)),
            dma((2, 5)),
            dma((2, 5)),
            held(OUT_ROWS, 1152),
            held(OUT_ROWS, 1024),
            held(IN_ROWS, 1152),
            held(IN_ROWS, 1024),
            held(IN_ROWS, 1024),
            held(IN_ROWS, 1024),
            held(OUT_ROWS, 1024),
            held(OUT_ROWS, 1024),
            held(288, 2048),
            held(288, 1024),
            held(288, 1024),
            held(288, 1024),
            held(288, 1024),
            held(288, 3072),
            held(288, 1024),
            held(288, 1024),
            held(288, 3072),
            held(288, 1024, dtype=F32),
            held(288, 2048, dtype=F32),
            held(12, 16, 384, dtype=F32),
            held(48, 640),
            held(16, 144, 144, dtype=F32),
            held(2, 144, 144, dtype=F32),
            held(16, 128, dtype=F32),
        ],
        compiler_params=pltpu.CompilerParams(
            collective_id=0, has_side_effects=True, vmem_limit_bytes=56 << 20
        ),
        cost_estimate=pl.CostEstimate(
            flops=10_000_000_000, bytes_accessed=20_000_000, transcendentals=700_000
        ),
    )(
        fine.reshape(1152, 512),
        merge_gain.reshape(1, 2048),
        merge_w,
        attn_gain.reshape(1, 1024),
        qkv_w,
        proj_w,
        table,
        region,
        counts,
        cot.reshape(288, 1024),
    )
    return out.reshape(12, 24, 1024), grad_fine.reshape(24, 48, 512)


def solution(mesh):
    grid = P("lat", "lon", None)
    rows = P("lat", None)
    return jax.shard_map(
        local,
        mesh=mesh,
        in_specs=(grid, P(), rows, P(), rows, rows, P(), P("lat", "lon"), P(), grid),
        out_specs=(grid, grid),
        check_vma=False,
    )
```

```python
import functools

import jax
import jax.numpy as jnp
from jax import lax
from jax.experimental import pallas as pl
from jax.experimental.pallas import tpu as pltpu
from jax.sharding import PartitionSpec as P

MESH = pl.DeviceIdType.MESH
BF16 = jnp.bfloat16
F32 = jnp.float32
NORM_EPS = 1e-05
MASKED = -1000000000.0
NT = (((1,), (1,)), ((), ()))
TN = (((0,), (0,)), ((), ()))

KEYS = [(1, 0), (0, 3), (0, 1), (0, 2), (1, 3), (1, 1), (1, 2)]
CROSS = [(1, 0), (0, 3), (0, 1), (0, 2, 0), (0, 2, 1), (1, 3), (1, 1), (1, 2)]
RID = {("c",) + k: i for i, k in enumerate(CROSS)}
RID.update({("r",) + k: 8 + i for i, k in enumerate(KEYS)})
RID.update({("k",) + k: 15 + i for i, k in enumerate(KEYS)})
RID.update({("q",) + k: 22 + i for i, k in enumerate(KEYS)})
RID[("own",)] = 29
N_IDS = 30
OWN = 7
PLAN = [
    (0, 7, "ym"), (0, 7, "yp"), (0, 7, "xh"), (1, 7, "xh"), (2, 7, "xh"), (1, 7, "ym"), (1, 7, "core"), (1, 7, "yp"),
    (0, 1, "yp"), (0, 0, "yp"), (0, 2, "ym"), (0, 1, "zm"), (0, 0, "ym"), (0, 0, "zp"), (0, 2, "xl"), (2, 7, "yp"),
    (1, 0, "zm"), (0, 2, "core"), (1, 1, "yp"), (1, 2, "ym"), (1, 2, "zp"), (1, 0, "ym"), (1, 1, "xl"),
    (0, 9, "core"), (2, 0, "core"), (0, 3, "xl"), (0, 0, "core"), (0, 3, "xh"), (0, 3, "core"), "tag", (2, 7, "ym"),
    (2, 0, "yp"), "bl0", (0, 5, "zp"), (0, 1, "core"), (0, 4, "zm"), "pat1", (2, 0, "xl"), (1, 2, "core"),
    (2, 1, "yp"), (0, 4, "core"), (1, 1, "core"), (0, 8, "core"), (1, 0, "yp"), "Hc", "bl1", (0, 6, "zp"), "bl2",
    (1, 3, "xh"), (1, 3, "zp"), (0, 6, "core"), (0, 7, "core"), "pat2", (1, 10, "core"), (0, 13, "core"),
    (0, 12, "core"), (0, 5, "core"), (2, 4, "xl"), (0, 11, "core"), (1, 5, "zm"), (0, 14, "core"), (0, 10, "core"),
    (2, 2, "ym"), "pat0", (2, 2, "xl"), (2, 2, "core"), (2, 4, "core"), (1, 6, "zp"), (2, 8, "core"), (1, 9, "core"),
    (1, 6, "core"), (2, 7, "core"), (1, 4, "zm"), (2, 3, "zp"), (1, 8, "core"), (2, 3, "xh"), "fin0", (1, 5, "core"),
    (2, 0, "ym"), (1, 3, "core"), "merge", "Hm", (1, 4, "core"), (1, 0, "core"), (2, 5, "zm"), (2, 12, "core"),
    (2, 1, "zp"), (1, 13, "core"), (2, 1, "core"), "wHc", (2, 3, "core"), "basm", (1, 14, "core"), (1, 12, "core"),
    (2, 6, "xl"), (1, 11, "core"), "wincot", (2, 11, "core"), (2, 5, "core"), (2, 6, "core"), (2, 9, "core"), "wHm",
    (2, 10, "core"), "winmer", "fin1", (2, 14, "core"), (2, 13, "core"), "qkv", "fin2", "up",
]

TC, TL, BR, BL, BLX = 0, 1, 2, 3, 4
SLOT = ((0, 80), (80, 48), (128, 48), (176, 48), (224, 48))
IN_ROWS, OUT_ROWS = 272, 224


class Gather:
    def __init__(self, shards, fulls, send_sem, recv_sem, local_sem):
        self.shards, self.fulls = shards, fulls
        self.send_sem, self.recv_sem, self.local_sem = send_sem, recv_sem, local_sem
        lat, lon = lax.axis_index("lat"), lax.axis_index("lon")
        a, y, k = lat // 8, (lat // 2) % 4, lat % 2
        z, xlo = lon // 2, lon % 2
        self.a, self.y, self.k = a, y, k
        self.c = (xlo + a + z) % 2

        def at(a_, y_, k_):
            return a_ * 8 + y_ * 2 + k_

        self.near = dict(
            yp=(at(a, (y + 1) % 4, k), lon),
            ym=(at(a, (y + 3) % 4, k), lon),
            xh=(at(1 - a, y, k), z * 2 + (1 - xlo)),
            xl=(lat, z * 2 + (1 - xlo)),
            zp=(lat, ((z + 1) % 8) * 2 + xlo),
            zm=(lat, ((z + 7) % 8) * 2 + xlo),
            core=(at(a, y, 1 - k), lon),
        )
        self.sent, self.local, self.here = [], {}, set()
        self.count = [0] * len(shards)

    def rows(self, w, key, half, core):
        r = self.shards[w].shape[0]
        a = self.a if key[0] == 0 else 1 - self.a
        s = a * 8 + ((self.y + key[1]) % 4) * 2 + core
        if half is None:
            return pl.ds(pl.multiple_of(s * r, r), r)
        off, n = half * (r // 2), r // 2
        if len(key) == 3:
            off, n = off + key[2] * (r // 4), r // 4
        return pl.ds(pl.multiple_of(s * r + off, n), n)

    def copy(self, w, rid, src, dst, dev, i):
        return pltpu.make_async_remote_copy(
            src_ref=src,
            dst_ref=dst,
            send_sem=self.send_sem.at[w, i],
            recv_sem=self.recv_sem.at[w, RID[rid]],
            device_id=dev,
            device_id_type=MESH,
        )

    def send(self, w, where, to, rid, src=None):
        full = self.fulls[w]
        i = self.count[w]
        self.count[w] += 1
        src = full.at[where] if src is None else src
        cp = self.copy(w, rid, src, full.at[where], self.near[to], i)
        cp.start()
        self.sent.append(cp)

    def recv(self, w, rid, where):
        part = self.fulls[w].at[where]
        self.copy(w, rid, part, part, self.near["core"], 0).wait_recv()

    def source(self, w, src):
        if src == OWN:
            return self.rows(w, (0, 0), None, self.k)
        key = KEYS[src % 8]
        half = self.c if src < 8 else 1 - self.c
        where = self.rows(w, key, half, self.k)
        if (w, src) not in self.here:
            self.here.add((w, src))
            if src >= 8:
                self.recv(w, ("r",) + key, where)
            elif key == (0, 2):
                for part in (0, 1):
                    self.recv(w, ("c", 0, 2, part), self.rows(w, (0, 2, part), half, self.k))
            else:
                self.recv(w, ("c",) + key, where)
        return where

    def hop(self, w, src, to):
        c, k = self.c, self.k
        where = self.source(w, src)
        if src == OWN:
            shard = self.shards[w]
            r = shard.shape[0] // 2
            if to == "core":
                self.send(w, where, to, ("own",), shard)
                cp = pltpu.make_async_copy(shard, self.fulls[w].at[where], self.local_sem.at[w])
                cp.start()
                self.local[w] = cp
            else:
                half = shard.at[pl.ds(pl.multiple_of(c * r, r), r)]
                rid = {"xh": (1, 0), "yp": (0, 3), "ym": (0, 1)}[to]
                self.send(w, self.rows(w, (0, 0), c, k), to, ("c",) + rid, half)
            return
        key = KEYS[src % 8]
        if to == "core":
            self.send(w, where, to, (("k",) if src < 8 else ("q",)) + key)
        elif to in ("zp", "zm", "xl"):
            self.send(w, where, to, ("r",) + key)
        elif key == (1, 0):
            self.send(w, where, to, ("c", 1, 3 if to == "yp" else 1))
        elif key == (0, 2):
            self.send(w, where, to, ("c", 1, 2))
        else:
            part = 0 if to == "yp" else 1
            self.send(w, self.rows(w, key + (part,), c, k), to, ("c", 0, 2, part))

    def fin(self, w):
        self.recv(w, ("own",), self.rows(w, (0, 0), None, 1 - self.k))
        for key in KEYS:
            self.recv(w, ("k",) + key, self.rows(w, key, self.c, 1 - self.k))
            self.recv(w, ("q",) + key, self.rows(w, key, 1 - self.c, 1 - self.k))
        self.local[w].wait()

    def drain(self):
        for cp in self.sent:
            cp.wait_send()


def over12(v):
    return (v * 171) >> 11


def over6(v):
    return (v * 171) >> 10


def window_source(d, lat):
    second = d >= 144
    e = jnp.where(second, d - 144, d)
    r = over12(e)
    c = e - 12 * r
    none = jnp.full(d.shape, -1, jnp.int32)
    lats = jnp.zeros(d.shape, jnp.int32) + lat
    upper = r < 6
    left = c < 6
    edge = (r - 6) * 6 + (c - 6)
    last = lats == 15
    first = lats == 0
    own_a = jnp.where(upper, (6 + r) * 24 + 6 + c, jnp.where(last & left, r * 24 + 18 + c, none))
    in_a = jnp.where(
        upper,
        none,
        jnp.where(last, jnp.where(left, none, SLOT[BLX][0] + edge), (r - 6) * 12 + c),
    )
    own_b = jnp.where(
        upper,
        jnp.where(first, r * 24 + 6 + c, none),
        jnp.where(left, (r - 6) * 24 + 18 + c, none),
    )
    in_top = jnp.where(left, SLOT[BR][0] + r * 6 + c, SLOT[BL][0] + r * 6 + c - 6)
    in_b = jnp.where(
        upper,
        jnp.where(first, none, in_top),
        jnp.where(left, none, SLOT[TL][0] + edge),
    )
    return jnp.where(second, own_b, own_a), jnp.where(second, in_b, in_a)


def slot_source(s):
    none = jnp.full(s.shape, -1, jnp.int32)
    r12 = over12(s)
    tc = jnp.where(s < 72, r12 * 24 + 6 + s - 12 * r12, none)

    def corner(base, row, col):
        t = s - base
        r = over6(t)
        return jnp.where(t < 36, (row + r) * 24 + col + t - 6 * r, none)

    tl, br, bl = corner(80, 0, 0), corner(128, 6, 18), corner(176, 6, 0)
    return jnp.where(s < 80, tc, jnp.where(s < 128, tl, jnp.where(s < 176, br, bl)))


def column(n):
    return lax.broadcasted_iota(jnp.int32, (n, 1), 0)


def line(n):
    return lax.broadcasted_iota(jnp.int32, (1, n), 1)


def pick(source, rows, cols):
    axis = 1 if source.shape[1] == 1 else 0
    place = lax.broadcasted_iota(jnp.int32, (rows, cols), axis)
    return (source == place).astype(F32).astype(BF16)


def dot(a, b):
    return jnp.dot(a, b, preferred_element_type=F32)


def dot_nt(a, b):
    return lax.dot_general(a, b, NT, preferred_element_type=F32)


def dot_tn(a, b):
    return lax.dot_general(a, b, TN, preferred_element_type=F32)


def norm_rows(v):
    n = v.shape[-1]
    centred = v - jnp.sum(v, axis=-1, keepdims=True) * (1.0 / n)
    inv = lax.rsqrt(jnp.sum(centred * centred, axis=-1, keepdims=True) * (1.0 / n) + NORM_EPS)
    return centred * inv, inv


def kernel(
    fine_hbm,
    merge_gain_hbm,
    merge_shard,
    attn_gain_hbm,
    qkv_shard,
    proj_shard,
    table_hbm,
    region_hbm,
    counts_hbm,
    cot_hbm,
    out,
    grad_fine,
    merge,
    qkv_w,
    proj,
    g_send,
    g_recv,
    g_local,
    f_send,
    f_recv,
    b_send,
    b_recv,
    out_cot,
    out_mer,
    in_cot,
    in_mer,
    back_out,
    back_grad,
    home_out,
    home_grad,
    patch_n,
    patch_f,
    patch_inv,
    merged_home,
    win_mer,
    win_cot,
    normed,
    proj_all,
    upstream,
    attended,
    grad_all,
    wide,
    grad_patch,
    lines,
    split,
    bias,
    mask,
    tag_pad,
    live,
    fine,
    cot,
    merge_gain,
    attn_gain,
    table,
    region,
    counts,
    load_sem,
    score_buf,
    grads_buf,
    low_buf,
    logit_buf,
):
    lat, lon = lax.axis_index("lat"), lax.axis_index("lon")
    up = ((lat + 15) % 16, lon)
    down = ((lat + 1) % 16, lon)
    left = (lat, (lon + 15) % 16)
    right = (lat, (lon + 1) % 16)
    down_left = ((lat + 1) % 16, (lon + 15) % 16)
    up_right = ((lat + 15) % 16, (lon + 1) % 16)
    gather = Gather((merge_shard, qkv_shard, proj_shard), (merge, qkv_w, proj), g_send, g_recv, g_local)

    pairs = dict(
        region=(region_hbm, region),
        counts=(counts_hbm, counts),
        cot=(cot_hbm, cot),
        fine=(fine_hbm, fine),
        merge_gain=(merge_gain_hbm, merge_gain),
        table=(table_hbm, table),
        attn_gain=(attn_gain_hbm, attn_gain),
    )
    loads = {
        name: pltpu.make_async_copy(src, dst, load_sem.at[i])
        for i, (name, (src, dst)) in enumerate(pairs.items())
    }
    for cp in loads.values():
        cp.start()

    def loaded(*names):
        for name in names:
            if name in loads:
                loads.pop(name).wait()

    for ref in (in_cot, in_mer, home_out, home_grad):
        ref[...] = jnp.zeros_like(ref)
    barrier = pltpu.get_barrier_semaphore()
    partners = list(gather.near.values()) + [up, down, left, right, down_left, up_right]
    for dev in partners:
        pl.semaphore_signal(barrier, inc=1, device_id=dev, device_id_type=MESH)
    pl.semaphore_wait(barrier, len(partners))

    not_first, not_last, is_last = lat > 0, lat < 15, lat == 15

    def forward(m, src, dst, do):
        def go(slot_from, slot_to, dev):
            f0, n = SLOT[slot_from]
            t0 = SLOT[slot_to][0]
            do(
                pltpu.make_async_remote_copy(
                    src_ref=src.at[pl.ds(f0, n)],
                    dst_ref=dst.at[pl.ds(t0, n)],
                    send_sem=f_send.at[m, slot_from],
                    recv_sem=f_recv.at[m, slot_to],
                    device_id=dev,
                    device_id_type=MESH,
                )
            )

        go(TL, TL, left)

        @pl.when(not_first)
        def _():
            go(TC, TC, up)

        @pl.when(not_last)
        def _():
            go(BR, BR, down)
            go(BL, BL, down_left)

        @pl.when(is_last)
        def _():
            go(BL, BLX, left)

    def forward_recv(m, dst):
        def got(slot):
            f0, n = SLOT[slot]
            part = dst.at[pl.ds(f0, n)]
            pltpu.make_async_remote_copy(
                src_ref=part,
                dst_ref=part,
                send_sem=f_send.at[m, 0],
                recv_sem=f_recv.at[m, slot],
                device_id=right,
                device_id_type=MESH,
            ).wait_recv()

        got(TL)

        @pl.when(not_last)
        def _():
            got(TC)

        @pl.when(not_first)
        def _():
            got(BR)
            got(BL)

        @pl.when(is_last)
        def _():
            got(BLX)

    def backward(m, w, src, dst, do):
        def go(slot_from, slot_to, dev):
            f0, n = SLOT[slot_from]
            t0 = SLOT[slot_to][0]
            do(
                pltpu.make_async_remote_copy(
                    src_ref=src.at[pl.ds(f0, n)],
                    dst_ref=dst.at[pl.ds(t0, n)],
                    send_sem=b_send.at[m, slot_from],
                    recv_sem=b_recv.at[m, slot_to],
                    device_id=dev,
                    device_id_type=MESH,
                )
            )

        if w == 1:
            go(TL, TL, right)

            @pl.when(not_first)
            def _():
                go(BL, BL, up_right)
                go(BR, BR, up)

        else:

            @pl.when(not_last)
            def _():
                go(TC, TC, down)

            @pl.when(is_last)
            def _():
                go(BLX, BL, right)

    def backward_recv(m, dst):
        def got(slot):
            f0, n = SLOT[slot]
            part = dst.at[pl.ds(f0, n)]
            pltpu.make_async_remote_copy(
                src_ref=part,
                dst_ref=part,
                send_sem=b_send.at[m, 0],
                recv_sem=b_recv.at[m, slot],
                device_id=right,
                device_id_type=MESH,
            ).wait_recv()

        got(TL)
        got(BL)

        @pl.when(not_first)
        def _():
            got(TC)

        @pl.when(not_last)
        def _():
            got(BR)

    def start(cp):
        cp.start()

    def sent(cp):
        cp.wait_send()

    cell = column(288)
    cell_row = (cell * 171) >> 12
    v = {}

    def step_tag():
        loaded("region", "counts", "cot")
        tag_pad[...] = jnp.zeros_like(tag_pad)
        tag_pad[0:12, 0:24] = (region[...] + 1).astype(F32)
        cell_col = cell - 24 * cell_row
        row_pick = (cell_row == lax.broadcasted_iota(jnp.int32, (288, 16), 1)).astype(F32).astype(BF16)
        tags = dot(row_pick, tag_pad[...].astype(BF16))
        lanes128 = lax.broadcasted_iota(jnp.int32, (288, 128), 1)
        tag = jnp.sum(jnp.where(lanes128 == cell_col, tags, 0.0), axis=-1, keepdims=True)
        held_rows = jnp.sum(jnp.where(line(16) == lat, counts[...], 0), axis=-1, keepdims=True)
        tag = tag * (cell_row < held_rows).astype(F32)
        v["tag_home"] = jnp.broadcast_to(tag, (288, 128)).astype(BF16)
        v["to_slots"] = pick(slot_source(column(OUT_ROWS)), OUT_ROWS, 288)
        out_cot[:, 0:1024] = dot(v["to_slots"], cot[...]).astype(BF16)
        out_cot[:, 1024:1152] = dot(v["to_slots"], v["tag_home"]).astype(BF16)

    def step_send_cot():
        forward(0, out_cot, in_cot, start)

    o = column(192)
    block = jnp.where(o < 48, 0, jnp.where(o < 96, 1, jnp.where(o < 144, 2, 3)))
    within = o - 48 * block
    wr = (within >= 24).astype(jnp.int32)
    wc = within - 24 * wr
    to_blocks = pick((2 * wr + (block & 1)) * 48 + 2 * wc + (block >> 1), 192, 192)

    def patches(g, _):
        raw = dot(to_blocks, fine[pl.ds(pl.multiple_of(g * 192, 192), 192), :])
        parts = [raw[48 * b : 48 * b + 48] for b in range(4)]
        average = sum(jnp.sum(p, axis=-1, keepdims=True) for p in parts) * (1.0 / 2048)
        parts = [p - average for p in parts]
        spread = sum(jnp.sum(p * p, axis=-1, keepdims=True) for p in parts) * (1.0 / 2048)
        inv = lax.rsqrt(spread + NORM_EPS)
        at = pl.ds(pl.multiple_of(g * 48, 48), 48)
        for b in range(4):
            gain = merge_gain[:, 512 * b : 512 * b + 512]
            normal = parts[b] * inv
            patch_f[at, 512 * b : 512 * b + 512] = normal
            patch_n[at, 512 * b : 512 * b + 512] = (normal * gain).astype(BF16)
        patch_inv[at, :] = jnp.broadcast_to(inv, (48, 128))
        return 0

    def step_patches(part):
        loaded("fine", "merge_gain")
        lax.fori_loop(2 * part, 2 * part + 2, patches, 0)

    def bias_lines(c, _):
        lane = line(384)
        u = over12(lane)
        index = jnp.where(lane < 276, u * 23 + (lane - 12 * u) - c + 11, -1)
        three = dot(split[...], pick(index, 640, 384))
        lines[c] = three[0:16] + three[16:32] + three[32:48]
        return 0

    def step_lines(part):
        if "table" in loads:
            loaded("table")
            t = table[...]
            high = t.astype(BF16)
            rest = t - high.astype(F32)
            middle = rest.astype(BF16)
            split[...] = jnp.zeros_like(split)
            split[0:16, 0:529] = high
            split[16:32, 0:529] = middle
            split[32:48, 0:529] = (rest - middle.astype(F32)).astype(BF16)
        lax.fori_loop(4 * part, 4 * part + 4, bias_lines, 0)

    def step_bias():
        for h in range(16):
            some = lines[:, h, :]
            for r in range(12):
                at = 144 * h + 12 * r
                bias[at : at + 12, :] = some[:, 12 * (11 - r) : 12 * (11 - r) + 144]

    def step_merge():
        def merge_tile(n, _):
            at = pl.ds(pl.multiple_of(n * 512, 512), 512)
            merged_home[:, at] = dot(patch_n[...], merge[:, at]).astype(BF16)
            return 0

        lax.fori_loop(0, 2, merge_tile, 0)
        out_mer[...] = dot(v["to_slots"], merged_home[...]).astype(BF16)

    def step_send_merged():
        forward(1, out_mer, in_mer, start)

    def owner():
        own, came = window_source(column(288), lat)
        return pick(own, 288, 288), pick(came, 288, IN_ROWS)

    def step_window_cot():
        from_home, from_slots = owner()
        win_cot[...] = (dot(from_home, cot[...]) + dot(from_slots, in_cot[:, 0:1024])).astype(BF16)
        win_tag = dot(from_home, v["tag_home"]) + dot(from_slots, in_cot[:, 1024:1152])
        d = lax.broadcasted_iota(jnp.int32, (288, 128), 0)
        apart = ((lat == 15) & (d >= 72) & (d < 144)) | ((lat == 0) & (d >= 144) & (d < 216))
        alive = (win_tag > 0).astype(F32)
        live[...] = alive
        win_tag = win_tag + 8.0 * alive * apart.astype(F32)
        for w in range(2):
            at = slice(144 * w, 144 * w + 144)
            key_tag = win_tag[at, 0:1]
            query_tag = jnp.transpose(win_tag[at])[0:1]
            allowed = (key_tag == query_tag) & (key_tag > 0)
            mask[w] = jnp.where(allowed, 0.0, MASKED)

    def step_window_merged():
        from_home, from_slots = owner()
        win_mer[...] = (dot(from_home, merged_home[...]) + dot(from_slots, in_mer[...])).astype(BF16)

        loaded("attn_gain")

        def norm_chunk(g, _):
            at = pl.ds(pl.multiple_of(g * 144, 144), 144)
            normed[at, :] = (norm_rows(win_mer[at, :].astype(F32))[0] * attn_gain[...]).astype(BF16)
            return 0

        lax.fori_loop(0, 2, norm_chunk, 0)

    def step_qkv():
        def qkv_tile(n, _):
            at = pl.ds(pl.multiple_of(n * 1024, 1024), 1024)
            proj_all[:, at] = dot(normed[...], qkv_w[:, at]).astype(BF16)
            return 0

        lax.fori_loop(0, 3, qkv_tile, 0)

    def step_upstream():
        upstream[...] = (dot_nt(win_cot[...], proj[...]) * live[:, 0:1]).astype(BF16)

    steps = dict(
        tag=step_tag,
        Hc=step_send_cot,
        pat0=lambda: step_patches(0),
        pat1=lambda: step_patches(1),
        pat2=lambda: step_patches(2),
        bl0=lambda: step_lines(0),
        bl1=lambda: step_lines(1),
        bl2=lambda: step_lines(2),
        basm=step_bias,
        fin0=lambda: gather.fin(0),
        fin1=lambda: gather.fin(1),
        fin2=lambda: gather.fin(2),
        merge=step_merge,
        Hm=step_send_merged,
        wHc=lambda: forward_recv(0, in_cot),
        wHm=lambda: forward_recv(1, in_mer),
        wincot=step_window_cot,
        winmer=step_window_merged,
        qkv=step_qkv,
        up=step_upstream,
    )
    for op in PLAN:
        if isinstance(op, str):
            steps[op]()
        else:
            gather.hop(*op)

    low_half = lax.broadcasted_iota(jnp.int32, (144, 128), 1) < 64
    none = jnp.zeros((144, 128), BF16)

    def window_rows(w):
        return pl.ds(144 * w, 144)

    def features(w, pair):
        off = pl.multiple_of(pair * 128, 128)
        rows = window_rows(w)
        q = proj_all[rows, pl.ds(off, 128)] * jnp.asarray(0.125, BF16)
        k = proj_all[rows, pl.ds(1024 + off, 128)]
        v_ = proj_all[rows, pl.ds(2048 + off, 128)]
        return q, k, v_, upstream[rows, pl.ds(off, 128)]

    def stage_products(w, pair, slot):
        q, k, v_, u = features(w, pair)
        two_k = jnp.concatenate([jnp.where(low_half, k, none), jnp.where(low_half, none, k)])
        two_v = jnp.concatenate([jnp.where(low_half, v_, none), jnp.where(low_half, none, v_)])
        score_buf[slot] = dot_nt(two_k, q)
        grads_buf[slot] = dot_nt(two_v, u)

    def stage_softmax(w, pair, slot):
        offsets = bias[pl.ds(pl.multiple_of(pair * 288, 288), 288), :]
        scores = (score_buf[slot] + offsets).reshape(2, 144, 144) + mask[w][None]
        powers = jnp.exp(scores - jnp.max(scores, axis=1, keepdims=True))
        probs = powers * (1.0 / jnp.sum(powers, axis=1, keepdims=True))
        grads = grads_buf[slot].reshape(2, 144, 144)
        logits = probs * (grads - jnp.sum(probs * grads, axis=1, keepdims=True))
        low_buf[slot] = probs.astype(BF16).reshape(288, 144)
        logit_buf[slot] = logits.astype(BF16).reshape(288, 144)

    def stage_sums(w, pair, slot):
        off = pl.multiple_of(pair * 128, 128)
        rows = window_rows(w)
        q, k, v_, u = features(w, pair)
        low, logits = low_buf[slot], logit_buf[slot]

        def both(m, x):
            y = dot(m, x)
            return jnp.where(low_half, y[0:144], y[144:288])

        def turned(m):
            return jnp.concatenate([m[0:144].T, m[144:288].T])

        alive = live[144 * w : 144 * w + 144, :]
        attended[rows, pl.ds(off, 128)] = (both(turned(low), v_) * alive).astype(BF16)
        grad_all[rows, pl.ds(off, 128)] = (both(turned(logits), k) * 0.125).astype(BF16)
        grad_all[rows, pl.ds(1024 + off, 128)] = both(logits, q).astype(BF16)
        grad_all[rows, pl.ds(2048 + off, 128)] = both(low, u).astype(BF16)

    def pairs_of(w):
        def two(i, _):
            for b in range(2):
                j = 2 * i + b
                stage_sums(w, j, b)
                stage_softmax(w, j + 1, 1 - b)
                stage_products(w, j + 2, b)
            return 0

        lax.fori_loop(0, 3, two, 0)

    def slots_of(w):
        _, came = window_source(line(144) + 144 * w, lat)
        if w == 1:
            return pick(jnp.where(came >= 0, came - SLOT[TL][0], came), 144, 144)
        came = jnp.where(came >= SLOT[BLX][0], came - SLOT[BLX][0] + 80, came)
        return pick(came, 128, 144)

    def put_slots(w, dst, cells):
        moved = dot(slots_of(w), cells).astype(BF16)
        if w == 1:
            dst[80:224] = moved
        else:
            dst[0:80] = moved[0:80]
            dst[224:272] = moved[80:128]

    def window_tail(w):
        rows = window_rows(w)
        total = win_mer[rows, :].astype(F32) + dot(attended[rows, :], proj[...])
        normed[rows, :] = total.astype(BF16)
        put_slots(w, back_out, normed[rows, :])
        backward(0, w, back_out, home_out, start)
        for n in range(2):
            wide[rows, 512 * n : 512 * n + 512] = dot_nt(grad_all[rows, :], qkv_w[512 * n : 512 * n + 512, :])
        normal, inv = norm_rows(win_mer[rows, :].astype(F32))
        weighted = wide[rows, :] * attn_gain[...]
        first = jnp.sum(weighted, axis=-1, keepdims=True) * (1.0 / 1024)
        second = jnp.sum(weighted * normal, axis=-1, keepdims=True) * (1.0 / 1024)
        back = win_cot[rows, :].astype(F32) + inv * (weighted - first - normal * second)
        win_cot[rows, :] = back.astype(BF16)
        put_slots(w, back_grad, win_cot[rows, :])
        backward(1, w, back_grad, home_grad, start)

    stage_products(1, 0, 0)
    stage_products(1, 1, 1)
    stage_softmax(1, 0, 0)
    pairs_of(1)
    stage_sums(1, 6, 0)
    stage_softmax(1, 7, 1)
    stage_products(0, 0, 0)
    stage_sums(1, 7, 1)
    stage_softmax(0, 0, 0)
    stage_products(0, 1, 1)
    window_tail(1)
    pairs_of(0)
    stage_sums(0, 6, 0)
    stage_softmax(0, 7, 1)
    stage_sums(0, 7, 1)
    window_tail(0)

    own_l, _ = window_source(line(288), lat)
    to_home = pick(own_l, 288, 288)
    slots_home = pick(slot_source(line(OUT_ROWS)), 288, OUT_ROWS)
    backward_recv(0, home_out)
    out[...] = (dot(to_home, normed[...]) + dot(slots_home, home_out[...])).astype(BF16)
    backward_recv(1, home_grad)
    merged_home[...] = (dot(to_home, win_cot[...]) + dot(slots_home, home_grad[...])).astype(BF16)

    def patch_tile(n, _):
        at = pl.ds(pl.multiple_of(n * 1024, 1024), 1024)
        grad_patch[:, at] = dot_nt(merged_home[...], merge[at, :])
        return 0

    lax.fori_loop(0, 2, patch_tile, 0)

    def patch_back(g, _):
        at = pl.ds(pl.multiple_of(g * 48, 48), 48)
        parts = [patch_f[at, 512 * b : 512 * b + 512] for b in range(4)]
        inv = patch_inv[at, 0:1]
        weighted = [
            grad_patch[at, 512 * b : 512 * b + 512] * merge_gain[:, 512 * b : 512 * b + 512]
            for b in range(4)
        ]
        first = sum(jnp.sum(x, axis=-1, keepdims=True) for x in weighted) * (1.0 / 2048)
        second = sum(
            jnp.sum(x * n, axis=-1, keepdims=True) for x, n in zip(weighted, parts)
        ) * (1.0 / 2048)
        back = [(inv * (x - first - n * second)).astype(BF16) for x, n in zip(weighted, parts)]
        tokens = dot_tn(to_blocks, jnp.concatenate(back, axis=0))
        grad_fine[pl.ds(pl.multiple_of(g * 192, 192), 192), :] = tokens.astype(BF16)
        return 0

    lax.fori_loop(0, 6, patch_back, 0)

    gather.drain()
    forward(0, out_cot, in_cot, sent)
    forward(1, out_mer, in_mer, sent)
    for w in range(2):
        backward(0, w, back_out, home_out, sent)
        backward(1, w, back_grad, home_grad, sent)


def local(fine, merge_gain, merge_w, attn_gain, qkv_w, proj_w, table, region, counts, cot):
    whole = pl.BlockSpec(memory_space=pltpu.VMEM)
    away = pl.BlockSpec(memory_space=pl.ANY)
    dma = pltpu.SemaphoreType.DMA

    def held(*shape, dtype=BF16):
        return pltpu.VMEM(shape, dtype)

    out, grad_fine = pl.pallas_call(
        kernel,
        out_shape=[
            pltpu.VMEM((288, 1024), BF16),
            pltpu.VMEM((1152, 512), BF16),
        ],
        in_specs=[away] * 10,
        out_specs=[whole, whole],
        scratch_shapes=[
            held(2048, 1024),
            held(1024, 3072),
            held(1024, 1024),
            dma((3, N_IDS)),
            dma((3, N_IDS)),
            dma((3,)),
            dma((2, 5)),
            dma((2, 5)),
            dma((2, 5)),
            dma((2, 5)),
            held(OUT_ROWS, 1152),
            held(OUT_ROWS, 1024),
            held(IN_ROWS, 1152),
            held(IN_ROWS, 1024),
            held(IN_ROWS, 1024),
            held(IN_ROWS, 1024),
            held(OUT_ROWS, 1024),
            held(OUT_ROWS, 1024),
            held(288, 2048),
            held(288, 2048, dtype=F32),
            held(288, 128, dtype=F32),
            held(288, 1024),
            held(288, 1024),
            held(288, 1024),
            held(288, 1024),
            held(288, 3072),
            held(288, 1024),
            held(288, 1024),
            held(288, 3072),
            held(288, 1024, dtype=F32),
            held(288, 2048, dtype=F32),
            held(12, 16, 384, dtype=F32),
            held(48, 640),
            held(2304, 144, dtype=F32),
            held(2, 144, 144, dtype=F32),
            held(16, 128, dtype=F32),
            held(288, 128, dtype=F32),
            held(1152, 512),
            held(288, 1024),
            held(1, 2048, dtype=F32),
            held(1, 1024, dtype=F32),
            held(16, 529, dtype=F32),
            held(12, 24, dtype=jnp.int32),
            held(1, 16, dtype=jnp.int32),
            dma((7,)),
            held(2, 288, 144, dtype=F32),
            held(2, 288, 144, dtype=F32),
            held(2, 288, 144),
            held(2, 288, 144),
        ],
        compiler_params=pltpu.CompilerParams(
            collective_id=0, has_side_effects=True, vmem_limit_bytes=60 << 20
        ),
        cost_estimate=pl.CostEstimate(
            flops=10_000_000_000, bytes_accessed=20_000_000, transcendentals=700_000
        ),
    )(
        fine.reshape(1152, 512),
        merge_gain.reshape(1, 2048),
        merge_w,
        attn_gain.reshape(1, 1024),
        qkv_w,
        proj_w,
        table,
        region,
        counts.reshape(1, 16),
        cot.reshape(288, 1024),
    )
    return out.reshape(12, 24, 1024), grad_fine.reshape(24, 48, 512)


def solution(mesh):
    grid = P("lat", "lon", None)
    rows = P("lat", None)
    return jax.shard_map(
        local,
        mesh=mesh,
        in_specs=(grid, P(), rows, P(), rows, rows, P(), P("lat", "lon"), P(), grid),
        out_specs=(grid, grid),
        check_vma=False,
    )
```

```python
import functools

import jax
import jax.numpy as jnp
from jax import lax
from jax.experimental import pallas as pl
from jax.experimental.pallas import tpu as pltpu
from jax.sharding import PartitionSpec as P

MESH = pl.DeviceIdType.MESH
BF16 = jnp.bfloat16
F32 = jnp.float32
NORM_EPS = 1e-05
MASKED = -1000000000.0
NT = (((1,), (1,)), ((), ()))
TN = (((0,), (0,)), ((), ()))

KEYS = [(1, 0), (0, 3), (0, 1), (0, 2), (1, 3), (1, 1), (1, 2)]
CROSS = [(1, 0), (0, 3), (0, 1), (0, 2, 0), (0, 2, 1), (1, 3), (1, 1), (1, 2)]
RID = {("c",) + k: i for i, k in enumerate(CROSS)}
RID.update({("r",) + k: 8 + i for i, k in enumerate(KEYS)})
RID.update({("k",) + k: 15 + i for i, k in enumerate(KEYS)})
RID.update({("q",) + k: 22 + i for i, k in enumerate(KEYS)})
RID[("own",)] = 29
N_IDS = 30
OWN = 7
PLAN = [
    (0, 7, "ym"), (2, 7, "xh"), (2, 7, "core"), (0, 7, "yp"), (1, 7, "yp"), (0, 7, "xh"), (1, 7, "xh"), (1, 7, "ym"),
    (0, 2, "zm"), "bl2", (0, 2, "ym"), (0, 1, "xl"), (0, 1, "yp"), (0, 0, "ym"), (0, 0, "yp"), (2, 7, "yp"),
    (0, 0, "zp"), "tag", (1, 2, "zp"), (2, 7, "ym"), (1, 1, "core"), (1, 1, "xl"), (0, 3, "xh"), (0, 1, "core"),
    (0, 3, "zm"), (2, 0, "core"), (0, 9, "core"), "pat0", (1, 2, "core"), (1, 7, "core"), (1, 1, "yp"), (1, 2, "ym"),
    (1, 0, "yp"), (2, 0, "yp"), (0, 5, "zp"), (0, 4, "zm"), (0, 0, "core"), (2, 0, "xl"), (0, 2, "core"), "pat2",
    (2, 2, "ym"), (1, 0, "zp"), (0, 6, "xl"), (2, 2, "core"), (1, 0, "ym"), (0, 11, "core"), (1, 3, "zm"),
    (0, 7, "core"), (0, 8, "core"), (2, 1, "core"), (0, 4, "core"), (0, 3, "core"), (2, 1, "yp"), (0, 6, "core"),
    (1, 3, "xh"), "Hc", (1, 9, "core"), (0, 10, "core"), (0, 12, "core"), (0, 5, "core"), (0, 13, "core"), "pat1",
    (2, 0, "ym"), (0, 14, "core"), (2, 1, "zp"), (1, 4, "zp"), "fin0", (1, 5, "zm"), (1, 4, "core"), "merge",
    (1, 6, "core"), (2, 3, "xh"), "Hm", (1, 0, "core"), (2, 2, "xl"), (1, 6, "zp"), "bl0", (1, 5, "core"),
    (1, 8, "core"), (2, 8, "core"), (2, 3, "core"), (2, 4, "core"), "bl1", (1, 10, "core"), (2, 4, "zp"), "wHc",
    (2, 3, "zm"), (1, 13, "core"), (2, 6, "core"), (1, 12, "core"), "basm", (2, 5, "zm"), (2, 6, "xl"),
    (1, 11, "core"), "wincot", (1, 3, "core"), (1, 14, "core"), (2, 9, "core"), (2, 10, "core"), "wHm",
    (2, 5, "core"), (2, 11, "core"), "winmer", (2, 13, "core"), (2, 14, "core"), "fin1", (2, 12, "core"), "qkv",
    "fin2", "up",
]

TC, TL, BR, BL, BLX = 0, 1, 2, 3, 4
SLOT = ((0, 80), (80, 48), (128, 48), (176, 48), (224, 48))
IN_ROWS, OUT_ROWS = 272, 224


class Gather:
    def __init__(self, shards, fulls, send_sem, recv_sem, local_sem):
        self.shards, self.fulls = shards, fulls
        self.send_sem, self.recv_sem, self.local_sem = send_sem, recv_sem, local_sem
        lat, lon = lax.axis_index("lat"), lax.axis_index("lon")
        a, y, k = lat // 8, (lat // 2) % 4, lat % 2
        z, xlo = lon // 2, lon % 2
        self.a, self.y, self.k = a, y, k
        self.c = (xlo + a + z) % 2

        def at(a_, y_, k_):
            return a_ * 8 + y_ * 2 + k_

        self.near = dict(
            yp=(at(a, (y + 1) % 4, k), lon),
            ym=(at(a, (y + 3) % 4, k), lon),
            xh=(at(1 - a, y, k), z * 2 + (1 - xlo)),
            xl=(lat, z * 2 + (1 - xlo)),
            zp=(lat, ((z + 1) % 8) * 2 + xlo),
            zm=(lat, ((z + 7) % 8) * 2 + xlo),
            core=(at(a, y, 1 - k), lon),
        )
        self.sent, self.local, self.here = [], {}, set()
        self.count = [0] * len(shards)

    def rows(self, w, key, half, core):
        r = self.shards[w].shape[0]
        a = self.a if key[0] == 0 else 1 - self.a
        s = a * 8 + ((self.y + key[1]) % 4) * 2 + core
        if half is None:
            return pl.ds(pl.multiple_of(s * r, r), r)
        off, n = half * (r // 2), r // 2
        if len(key) == 3:
            off, n = off + key[2] * (r // 4), r // 4
        return pl.ds(pl.multiple_of(s * r + off, n), n)

    def copy(self, w, rid, src, dst, dev, i):
        return pltpu.make_async_remote_copy(
            src_ref=src,
            dst_ref=dst,
            send_sem=self.send_sem.at[w, i],
            recv_sem=self.recv_sem.at[w, RID[rid]],
            device_id=dev,
            device_id_type=MESH,
        )

    def send(self, w, where, to, rid, src=None):
        full = self.fulls[w]
        i = self.count[w]
        self.count[w] += 1
        src = full.at[where] if src is None else src
        cp = self.copy(w, rid, src, full.at[where], self.near[to], i)
        cp.start()
        self.sent.append(cp)

    def recv(self, w, rid, where):
        part = self.fulls[w].at[where]
        self.copy(w, rid, part, part, self.near["core"], 0).wait_recv()

    def source(self, w, src):
        if src == OWN:
            return self.rows(w, (0, 0), None, self.k)
        key = KEYS[src % 8]
        half = self.c if src < 8 else 1 - self.c
        where = self.rows(w, key, half, self.k)
        if (w, src) not in self.here:
            self.here.add((w, src))
            if src >= 8:
                self.recv(w, ("r",) + key, where)
            elif key == (0, 2):
                for part in (0, 1):
                    self.recv(w, ("c", 0, 2, part), self.rows(w, (0, 2, part), half, self.k))
            else:
                self.recv(w, ("c",) + key, where)
        return where

    def hop(self, w, src, to):
        c, k = self.c, self.k
        where = self.source(w, src)
        if src == OWN:
            shard = self.shards[w]
            r = shard.shape[0] // 2
            if to == "core":
                self.send(w, where, to, ("own",), shard)
                cp = pltpu.make_async_copy(shard, self.fulls[w].at[where], self.local_sem.at[w])
                cp.start()
                self.local[w] = cp
            else:
                half = shard.at[pl.ds(pl.multiple_of(c * r, r), r)]
                rid = {"xh": (1, 0), "yp": (0, 3), "ym": (0, 1)}[to]
                self.send(w, self.rows(w, (0, 0), c, k), to, ("c",) + rid, half)
            return
        key = KEYS[src % 8]
        if to == "core":
            self.send(w, where, to, (("k",) if src < 8 else ("q",)) + key)
        elif to in ("zp", "zm", "xl"):
            self.send(w, where, to, ("r",) + key)
        elif key == (1, 0):
            self.send(w, where, to, ("c", 1, 3 if to == "yp" else 1))
        elif key == (0, 2):
            self.send(w, where, to, ("c", 1, 2))
        else:
            part = 0 if to == "yp" else 1
            self.send(w, self.rows(w, key + (part,), c, k), to, ("c", 0, 2, part))

    def fin(self, w):
        self.recv(w, ("own",), self.rows(w, (0, 0), None, 1 - self.k))
        for key in KEYS:
            self.recv(w, ("k",) + key, self.rows(w, key, self.c, 1 - self.k))
            self.recv(w, ("q",) + key, self.rows(w, key, 1 - self.c, 1 - self.k))
        self.local[w].wait()

    def drain(self):
        for cp in self.sent:
            cp.wait_send()


def over12(v):
    return (v * 171) >> 11


def over6(v):
    return (v * 171) >> 10


def window_source(d, lat):
    second = d >= 144
    e = jnp.where(second, d - 144, d)
    r = over12(e)
    c = e - 12 * r
    none = jnp.full(d.shape, -1, jnp.int32)
    lats = jnp.zeros(d.shape, jnp.int32) + lat
    upper = r < 6
    left = c < 6
    edge = (r - 6) * 6 + (c - 6)
    last = lats == 15
    first = lats == 0
    own_a = jnp.where(upper, (6 + r) * 24 + 6 + c, jnp.where(last & left, r * 24 + 18 + c, none))
    in_a = jnp.where(
        upper,
        none,
        jnp.where(last, jnp.where(left, none, SLOT[BLX][0] + edge), (r - 6) * 12 + c),
    )
    own_b = jnp.where(
        upper,
        jnp.where(first, r * 24 + 6 + c, none),
        jnp.where(left, (r - 6) * 24 + 18 + c, none),
    )
    in_top = jnp.where(left, SLOT[BR][0] + r * 6 + c, SLOT[BL][0] + r * 6 + c - 6)
    in_b = jnp.where(
        upper,
        jnp.where(first, none, in_top),
        jnp.where(left, none, SLOT[TL][0] + edge),
    )
    return jnp.where(second, own_b, own_a), jnp.where(second, in_b, in_a)


def slot_source(s):
    none = jnp.full(s.shape, -1, jnp.int32)
    r12 = over12(s)
    tc = jnp.where(s < 72, r12 * 24 + 6 + s - 12 * r12, none)

    def corner(base, row, col):
        t = s - base
        r = over6(t)
        return jnp.where(t < 36, (row + r) * 24 + col + t - 6 * r, none)

    tl, br, bl = corner(80, 0, 0), corner(128, 6, 18), corner(176, 6, 0)
    return jnp.where(s < 80, tc, jnp.where(s < 128, tl, jnp.where(s < 176, br, bl)))


def corner_split(t):
    c = (t >= 144).astype(jnp.int32) + (t >= 288) + (t >= 432)
    u = t - 144 * c
    q = (u >= 36).astype(jnp.int32) + (u >= 72) + (u >= 108)
    return 80 + 48 * c + u - 36 * q, q


def to_corner(slot, q):
    c = (slot >= 128).astype(jnp.int32) + (slot >= 176) + (slot >= 224)
    return jnp.where(slot >= 80, 96 * c + slot - 80 + 36 * q, -1)


def to_centre(slot, h):
    return jnp.where((slot >= 0) & (slot < 80), slot + 72 * h, -1)


def home_picks(t, u, shape):
    slot, q = corner_split(t)
    corner = slot_source(slot)
    h = (u >= 72).astype(jnp.int32)
    centre = slot_source(u - 72 * h)
    corners = [pick(jnp.where(q == i, corner, -1), *shape(432)) for i in range(4)]
    centres = [pick(jnp.where(h == i, centre, -1), *shape(144)) for i in range(2)]
    return corners, centres


def packed(picks, cells):
    width = 1024 // len(picks)
    parts = [dot(p, cells[:, width * i : width * i + width]) for i, p in enumerate(picks)]
    return sum(parts[1:], parts[0]).astype(BF16)


def unpacked(dst, rows, cells, corners, corner, centres, centre):
    for i in range(4):
        at = slice(256 * i, 256 * i + 256)
        half = slice(256 * (i % 2), 256 * (i % 2) + 256)
        total = dot(rows, cells[:, at]) + dot(corners[i], corner[...])
        dst[:, at] = (total + dot(centres[i // 2], centre[:, half])).astype(BF16)


def part_of(bufs, slot):
    if len(bufs) == 1:
        first, n = SLOT[slot]
        return bufs[0].at[pl.ds(first, n)]
    if slot == TC:
        return bufs[1].at[pl.ds(0, 144)]
    return bufs[0].at[pl.ds(144 * (slot - 1), 144)]


def column(n):
    return lax.broadcasted_iota(jnp.int32, (n, 1), 0)


def line(n):
    return lax.broadcasted_iota(jnp.int32, (1, n), 1)


def pick(source, rows, cols):
    axis = 1 if source.shape[1] == 1 else 0
    place = lax.broadcasted_iota(jnp.int32, (rows, cols), axis)
    return (source == place).astype(F32).astype(BF16)


def dot(a, b):
    return jnp.dot(a, b, preferred_element_type=F32)


def dot_nt(a, b):
    return lax.dot_general(a, b, NT, preferred_element_type=F32)


def dot_tn(a, b):
    return lax.dot_general(a, b, TN, preferred_element_type=F32)


def norm_rows(v):
    n = v.shape[-1]
    centred = v - jnp.sum(v, axis=-1, keepdims=True) * (1.0 / n)
    inv = lax.rsqrt(jnp.sum(centred * centred, axis=-1, keepdims=True) * (1.0 / n) + NORM_EPS)
    return centred * inv, inv


def kernel(
    fine_hbm,
    merge_gain_hbm,
    merge_shard,
    attn_gain_hbm,
    qkv_shard,
    proj_shard,
    table_hbm,
    region_hbm,
    counts_hbm,
    cot_hbm,
    out,
    grad_fine,
    merge,
    qkv_w,
    proj,
    g_send,
    g_recv,
    g_local,
    f_send,
    f_recv,
    b_send,
    b_recv,
    out_tag,
    in_tag,
    out_cot_c,
    out_cot_t,
    out_mer_c,
    out_mer_t,
    in_cot_c,
    in_cot_t,
    in_mer_c,
    in_mer_t,
    back_out_c,
    back_out_t,
    back_grad_c,
    back_grad_t,
    home_out_c,
    home_out_t,
    home_grad_c,
    home_grad_t,
    patch_n,
    patch_f,
    patch_inv,
    merged_home,
    win_mer,
    win_cot,
    normed,
    proj_all,
    upstream,
    attended,
    grad_all,
    wide,
    grad_patch,
    lines,
    split,
    bias,
    mask,
    tag_pad,
    live,
    fine,
    cot,
    merge_gain,
    attn_gain,
    table,
    region,
    counts,
    load_sem,
    score_buf,
    grads_buf,
    low_buf,
    logit_buf,
):
    lat, lon = lax.axis_index("lat"), lax.axis_index("lon")
    up = ((lat + 15) % 16, lon)
    down = ((lat + 1) % 16, lon)
    left = (lat, (lon + 15) % 16)
    right = (lat, (lon + 1) % 16)
    down_left = ((lat + 1) % 16, (lon + 15) % 16)
    up_right = ((lat + 15) % 16, (lon + 1) % 16)
    gather = Gather((merge_shard, qkv_shard, proj_shard), (merge, qkv_w, proj), g_send, g_recv, g_local)

    pairs = dict(
        region=(region_hbm, region),
        counts=(counts_hbm, counts),
        cot=(cot_hbm, cot),
        fine=(fine_hbm, fine),
        merge_gain=(merge_gain_hbm, merge_gain),
        table=(table_hbm, table),
        attn_gain=(attn_gain_hbm, attn_gain),
    )
    loads = {
        name: pltpu.make_async_copy(src, dst, load_sem.at[i])
        for i, (name, (src, dst)) in enumerate(pairs.items())
    }
    for cp in loads.values():
        cp.start()

    def loaded(*names):
        for name in names:
            if name in loads:
                loads.pop(name).wait()

    out_cot, out_mer = (out_cot_c, out_cot_t), (out_mer_c, out_mer_t)
    in_cot, in_mer = (in_cot_c, in_cot_t), (in_mer_c, in_mer_t)
    back_out, back_grad = (back_out_c, back_out_t), (back_grad_c, back_grad_t)
    home_out, home_grad = (home_out_c, home_out_t), (home_grad_c, home_grad_t)
    for ref in (in_tag,) + in_cot + in_mer + home_out + home_grad:
        ref[...] = jnp.zeros_like(ref)
    barrier = pltpu.get_barrier_semaphore()
    partners = list(gather.near.values()) + [up, down, left, right, down_left, up_right]
    for dev in partners:
        pl.semaphore_signal(barrier, inc=1, device_id=dev, device_id_type=MESH)
    pl.semaphore_wait(barrier, len(partners))

    not_first, not_last, is_last = lat > 0, lat < 15, lat == 15

    def forward(m, src, dst, do):
        def go(slot_from, slot_to, dev):
            do(
                pltpu.make_async_remote_copy(
                    src_ref=part_of(src, slot_from),
                    dst_ref=part_of(dst, slot_to),
                    send_sem=f_send.at[m, slot_from],
                    recv_sem=f_recv.at[m, slot_to],
                    device_id=dev,
                    device_id_type=MESH,
                )
            )

        go(TL, TL, left)

        @pl.when(not_first)
        def _():
            go(TC, TC, up)

        @pl.when(not_last)
        def _():
            go(BR, BR, down)
            go(BL, BL, down_left)

        @pl.when(is_last)
        def _():
            go(BL, BLX, left)

    def forward_recv(m, dst):
        def got(slot):
            part = part_of(dst, slot)
            pltpu.make_async_remote_copy(
                src_ref=part,
                dst_ref=part,
                send_sem=f_send.at[m, 0],
                recv_sem=f_recv.at[m, slot],
                device_id=right,
                device_id_type=MESH,
            ).wait_recv()

        got(TL)

        @pl.when(not_last)
        def _():
            got(TC)

        @pl.when(not_first)
        def _():
            got(BR)
            got(BL)

        @pl.when(is_last)
        def _():
            got(BLX)

    def backward(m, w, src, dst, do):
        def go(slot_from, slot_to, dev):
            do(
                pltpu.make_async_remote_copy(
                    src_ref=part_of(src, slot_from),
                    dst_ref=part_of(dst, slot_to),
                    send_sem=b_send.at[m, slot_from],
                    recv_sem=b_recv.at[m, slot_to],
                    device_id=dev,
                    device_id_type=MESH,
                )
            )

        if w == 1:
            go(TL, TL, right)

            @pl.when(not_first)
            def _():
                go(BL, BL, up_right)
                go(BR, BR, up)

        else:

            @pl.when(not_last)
            def _():
                go(TC, TC, down)

            @pl.when(is_last)
            def _():
                go(BLX, BL, right)

    def backward_recv(m, dst):
        def got(slot):
            part = part_of(dst, slot)
            pltpu.make_async_remote_copy(
                src_ref=part,
                dst_ref=part,
                send_sem=b_send.at[m, 0],
                recv_sem=b_recv.at[m, slot],
                device_id=right,
                device_id_type=MESH,
            ).wait_recv()

        got(TL)
        got(BL)

        @pl.when(not_first)
        def _():
            got(TC)

        @pl.when(not_last)
        def _():
            got(BR)

    def start(cp):
        cp.start()

    def sent(cp):
        cp.wait_send()

    cell = column(288)
    cell_row = (cell * 171) >> 12
    v = {}

    def step_tag():
        loaded("region", "counts", "cot")
        tag_pad[...] = jnp.zeros_like(tag_pad)
        tag_pad[0:12, 0:24] = (region[...] + 1).astype(F32)
        cell_col = cell - 24 * cell_row
        row_pick = (cell_row == lax.broadcasted_iota(jnp.int32, (288, 16), 1)).astype(F32).astype(BF16)
        tags = dot(row_pick, tag_pad[...].astype(BF16))
        lanes128 = lax.broadcasted_iota(jnp.int32, (288, 128), 1)
        tag = jnp.sum(jnp.where(lanes128 == cell_col, tags, 0.0), axis=-1, keepdims=True)
        held_rows = jnp.sum(jnp.where(line(16) == lat, counts[...], 0), axis=-1, keepdims=True)
        tag = tag * (cell_row < held_rows).astype(F32)
        v["tag_home"] = jnp.broadcast_to(tag, (288, 128)).astype(BF16)
        to_slots = pick(slot_source(column(OUT_ROWS)), OUT_ROWS, 288)
        out_tag[...] = dot(to_slots, v["tag_home"]).astype(BF16)
        v["out"] = home_picks(column(432), column(144), lambda n: (n, 288))
        out_cot_c[...] = packed(v["out"][0], cot)
        out_cot_t[...] = packed(v["out"][1], cot)

    def step_send_cot():
        forward(2, (out_tag,), (in_tag,), start)
        forward(0, out_cot, in_cot, start)

    o = column(192)
    block = jnp.where(o < 48, 0, jnp.where(o < 96, 1, jnp.where(o < 144, 2, 3)))
    within = o - 48 * block
    wr = (within >= 24).astype(jnp.int32)
    wc = within - 24 * wr
    to_blocks = pick((2 * wr + (block & 1)) * 48 + 2 * wc + (block >> 1), 192, 192)

    def patches(g, _):
        raw = dot(to_blocks, fine[pl.ds(pl.multiple_of(g * 192, 192), 192), :])
        parts = [raw[48 * b : 48 * b + 48] for b in range(4)]
        average = sum(jnp.sum(p, axis=-1, keepdims=True) for p in parts) * (1.0 / 2048)
        parts = [p - average for p in parts]
        spread = sum(jnp.sum(p * p, axis=-1, keepdims=True) for p in parts) * (1.0 / 2048)
        inv = lax.rsqrt(spread + NORM_EPS)
        at = pl.ds(pl.multiple_of(g * 48, 48), 48)
        for b in range(4):
            gain = merge_gain[:, 512 * b : 512 * b + 512]
            normal = parts[b] * inv
            patch_f[at, 512 * b : 512 * b + 512] = normal
            patch_n[at, 512 * b : 512 * b + 512] = (normal * gain).astype(BF16)
        patch_inv[at, :] = jnp.broadcast_to(inv, (48, 128))
        return 0

    def step_patches(part):
        loaded("fine", "merge_gain")
        lax.fori_loop(2 * part, 2 * part + 2, patches, 0)

    def bias_lines(c, _):
        lane = line(384)
        u = over12(lane)
        index = jnp.where(lane < 276, u * 23 + (lane - 12 * u) - c + 11, -1)
        three = dot(split[...], pick(index, 640, 384))
        lines[c] = three[0:16] + three[16:32] + three[32:48]
        return 0

    def step_lines(part):
        if "table" in loads:
            loaded("table")
            t = table[...]
            high = t.astype(BF16)
            rest = t - high.astype(F32)
            middle = rest.astype(BF16)
            split[...] = jnp.zeros_like(split)
            split[0:16, 0:529] = high
            split[16:32, 0:529] = middle
            split[32:48, 0:529] = (rest - middle.astype(F32)).astype(BF16)
        lax.fori_loop(4 * part, 4 * part + 4, bias_lines, 0)

    def step_bias():
        for h in range(16):
            some = lines[:, h, :]
            for r in range(12):
                at = 144 * h + 12 * r
                bias[at : at + 12, :] = some[:, 12 * (11 - r) : 12 * (11 - r) + 144]

    def step_merge():
        def merge_tile(n, _):
            at = pl.ds(pl.multiple_of(n * 512, 512), 512)
            merged_home[:, at] = dot(patch_n[...], merge[:, at]).astype(BF16)
            return 0

        lax.fori_loop(0, 2, merge_tile, 0)
        out_mer_c[...] = packed(v["out"][0], merged_home)
        out_mer_t[...] = packed(v["out"][1], merged_home)

    def step_send_merged():
        forward(1, out_mer, in_mer, start)

    def owner():
        own, came = window_source(column(288), lat)
        corners = [pick(to_corner(came, i), 288, 576) for i in range(4)]
        centres = [pick(to_centre(came, i), 288, 144) for i in range(2)]
        return pick(own, 288, 288), corners, centres, pick(came, 288, IN_ROWS)

    def step_window_cot():
        from_home, corners, centres, from_slots = owner()
        unpacked(win_cot, from_home, cot, corners, in_cot_c, centres, in_cot_t)
        win_tag = dot(from_home, v["tag_home"]) + dot(from_slots, in_tag[...])
        d = lax.broadcasted_iota(jnp.int32, (288, 128), 0)
        apart = ((lat == 15) & (d >= 72) & (d < 144)) | ((lat == 0) & (d >= 144) & (d < 216))
        alive = (win_tag > 0).astype(F32)
        live[...] = alive
        win_tag = win_tag + 8.0 * alive * apart.astype(F32)
        for w in range(2):
            at = slice(144 * w, 144 * w + 144)
            key_tag = win_tag[at, 0:1]
            query_tag = jnp.transpose(win_tag[at])[0:1]
            allowed = (key_tag == query_tag) & (key_tag > 0)
            mask[w] = jnp.where(allowed, 0.0, MASKED)

    def step_window_merged():
        from_home, corners, centres, _ = owner()
        unpacked(win_mer, from_home, merged_home, corners, in_mer_c, centres, in_mer_t)

        loaded("attn_gain")

        def norm_chunk(g, _):
            at = pl.ds(pl.multiple_of(g * 144, 144), 144)
            normed[at, :] = (norm_rows(win_mer[at, :].astype(F32))[0] * attn_gain[...]).astype(BF16)
            return 0

        lax.fori_loop(0, 2, norm_chunk, 0)

    def step_qkv():
        def qkv_tile(n, _):
            at = pl.ds(pl.multiple_of(n * 1024, 1024), 1024)
            proj_all[:, at] = dot(normed[...], qkv_w[:, at]).astype(BF16)
            return 0

        lax.fori_loop(0, 3, qkv_tile, 0)

    def step_upstream():
        upstream[...] = (dot_nt(win_cot[...], proj[...]) * live[:, 0:1]).astype(BF16)

    steps = dict(
        tag=step_tag,
        Hc=step_send_cot,
        pat0=lambda: step_patches(0),
        pat1=lambda: step_patches(1),
        pat2=lambda: step_patches(2),
        bl0=lambda: step_lines(0),
        bl1=lambda: step_lines(1),
        bl2=lambda: step_lines(2),
        basm=step_bias,
        fin0=lambda: gather.fin(0),
        fin1=lambda: gather.fin(1),
        fin2=lambda: gather.fin(2),
        merge=step_merge,
        Hm=step_send_merged,
        wHc=lambda: (forward_recv(2, (in_tag,)), forward_recv(0, in_cot)),
        wHm=lambda: forward_recv(1, in_mer),
        wincot=step_window_cot,
        winmer=step_window_merged,
        qkv=step_qkv,
        up=step_upstream,
    )
    for op in PLAN:
        if isinstance(op, str):
            steps[op]()
        else:
            gather.hop(*op)

    low_half = lax.broadcasted_iota(jnp.int32, (144, 128), 1) < 64
    none = jnp.zeros((144, 128), BF16)

    def window_rows(w):
        return pl.ds(144 * w, 144)

    def features(w, pair):
        off = pl.multiple_of(pair * 128, 128)
        rows = window_rows(w)
        q = proj_all[rows, pl.ds(off, 128)] * jnp.asarray(0.125, BF16)
        k = proj_all[rows, pl.ds(1024 + off, 128)]
        v_ = proj_all[rows, pl.ds(2048 + off, 128)]
        return q, k, v_, upstream[rows, pl.ds(off, 128)]

    def stage_products(w, pair, slot):
        q, k, v_, u = features(w, pair)
        two_k = jnp.concatenate([jnp.where(low_half, k, none), jnp.where(low_half, none, k)])
        two_v = jnp.concatenate([jnp.where(low_half, v_, none), jnp.where(low_half, none, v_)])
        score_buf[slot] = dot_nt(two_k, q)
        grads_buf[slot] = dot_nt(two_v, u)

    def stage_softmax(w, pair, slot):
        offsets = bias[pl.ds(pl.multiple_of(pair * 288, 288), 288), :]
        scores = (score_buf[slot] + offsets).reshape(2, 144, 144) + mask[w][None]
        powers = jnp.exp(scores - jnp.max(scores, axis=1, keepdims=True))
        probs = powers * (1.0 / jnp.sum(powers, axis=1, keepdims=True))
        grads = grads_buf[slot].reshape(2, 144, 144)
        logits = probs * (grads - jnp.sum(probs * grads, axis=1, keepdims=True))
        low_buf[slot] = probs.astype(BF16).reshape(288, 144)
        logit_buf[slot] = logits.astype(BF16).reshape(288, 144)

    def stage_sums(w, pair, slot):
        off = pl.multiple_of(pair * 128, 128)
        rows = window_rows(w)
        q, k, v_, u = features(w, pair)
        low, logits = low_buf[slot], logit_buf[slot]

        def both(m, x):
            y = dot(m, x)
            return jnp.where(low_half, y[0:144], y[144:288])

        def turned(m):
            return jnp.concatenate([m[0:144].T, m[144:288].T])

        alive = live[144 * w : 144 * w + 144, :]
        attended[rows, pl.ds(off, 128)] = (both(turned(low), v_) * alive).astype(BF16)
        grad_all[rows, pl.ds(off, 128)] = (both(turned(logits), k) * 0.125).astype(BF16)
        grad_all[rows, pl.ds(1024 + off, 128)] = both(logits, q).astype(BF16)
        grad_all[rows, pl.ds(2048 + off, 128)] = both(low, u).astype(BF16)

    def pairs_of(w):
        def two(i, _):
            for b in range(2):
                j = 2 * i + b
                stage_sums(w, j, b)
                stage_softmax(w, j + 1, 1 - b)
                stage_products(w, j + 2, b)
            return 0

        lax.fori_loop(0, 3, two, 0)

    def put_slots(w, bufs, cells):
        _, came = window_source(line(144) + 144 * w, lat)
        corner, centre = bufs
        if w == 1:
            corner[0:432] = packed([pick(to_corner(came, i), 432, 144) for i in range(4)], cells)
        else:
            last = [jnp.where(came >= SLOT[BLX][0], to_corner(came, i) - 432, -1) for i in range(4)]
            corner[432:576] = packed([pick(x, 144, 144) for x in last], cells)
            centre[...] = packed([pick(to_centre(came, i), 144, 144) for i in range(2)], cells)

    def window_tail(w):
        rows = window_rows(w)
        total = win_mer[rows, :].astype(F32) + dot(attended[rows, :], proj[...])
        normed[rows, :] = total.astype(BF16)
        put_slots(w, back_out, normed[rows, :])
        backward(0, w, back_out, home_out, start)
        for n in range(2):
            wide[rows, 512 * n : 512 * n + 512] = dot_nt(grad_all[rows, :], qkv_w[512 * n : 512 * n + 512, :])
        normal, inv = norm_rows(win_mer[rows, :].astype(F32))
        weighted = wide[rows, :] * attn_gain[...]
        first = jnp.sum(weighted, axis=-1, keepdims=True) * (1.0 / 1024)
        second = jnp.sum(weighted * normal, axis=-1, keepdims=True) * (1.0 / 1024)
        back = win_cot[rows, :].astype(F32) + inv * (weighted - first - normal * second)
        win_cot[rows, :] = back.astype(BF16)
        put_slots(w, back_grad, win_cot[rows, :])
        backward(1, w, back_grad, home_grad, start)

    stage_products(1, 0, 0)
    stage_products(1, 1, 1)
    stage_softmax(1, 0, 0)
    pairs_of(1)
    stage_sums(1, 6, 0)
    stage_softmax(1, 7, 1)
    stage_products(0, 0, 0)
    stage_sums(1, 7, 1)
    stage_softmax(0, 0, 0)
    stage_products(0, 1, 1)
    window_tail(1)
    pairs_of(0)
    stage_sums(0, 6, 0)
    stage_softmax(0, 7, 1)
    stage_sums(0, 7, 1)
    window_tail(0)

    own_l, _ = window_source(line(288), lat)
    to_home = pick(own_l, 288, 288)
    corners_home, centres_home = home_picks(line(432), line(144), lambda n: (288, n))
    backward_recv(0, home_out)
    unpacked(out, to_home, normed, corners_home, home_out_c, centres_home, home_out_t)
    backward_recv(1, home_grad)
    unpacked(merged_home, to_home, win_cot, corners_home, home_grad_c, centres_home, home_grad_t)

    def patch_tile(n, _):
        at = pl.ds(pl.multiple_of(n * 1024, 1024), 1024)
        grad_patch[:, at] = dot_nt(merged_home[...], merge[at, :])
        return 0

    lax.fori_loop(0, 2, patch_tile, 0)

    def patch_back(g, _):
        at = pl.ds(pl.multiple_of(g * 48, 48), 48)
        parts = [patch_f[at, 512 * b : 512 * b + 512] for b in range(4)]
        inv = patch_inv[at, 0:1]
        weighted = [
            grad_patch[at, 512 * b : 512 * b + 512] * merge_gain[:, 512 * b : 512 * b + 512]
            for b in range(4)
        ]
        first = sum(jnp.sum(x, axis=-1, keepdims=True) for x in weighted) * (1.0 / 2048)
        second = sum(
            jnp.sum(x * n, axis=-1, keepdims=True) for x, n in zip(weighted, parts)
        ) * (1.0 / 2048)
        back = [(inv * (x - first - n * second)).astype(BF16) for x, n in zip(weighted, parts)]
        tokens = dot_tn(to_blocks, jnp.concatenate(back, axis=0))
        grad_fine[pl.ds(pl.multiple_of(g * 192, 192), 192), :] = tokens.astype(BF16)
        return 0

    lax.fori_loop(0, 6, patch_back, 0)

    gather.drain()
    forward(2, (out_tag,), (in_tag,), sent)
    forward(0, out_cot, in_cot, sent)
    forward(1, out_mer, in_mer, sent)
    for w in range(2):
        backward(0, w, back_out, home_out, sent)
        backward(1, w, back_grad, home_grad, sent)


def local(fine, merge_gain, merge_w, attn_gain, qkv_w, proj_w, table, region, counts, cot):
    whole = pl.BlockSpec(memory_space=pltpu.VMEM)
    away = pl.BlockSpec(memory_space=pl.ANY)
    dma = pltpu.SemaphoreType.DMA

    def held(*shape, dtype=BF16):
        return pltpu.VMEM(shape, dtype)

    out, grad_fine = pl.pallas_call(
        kernel,
        out_shape=[
            pltpu.VMEM((288, 1024), BF16),
            pltpu.VMEM((1152, 512), BF16),
        ],
        in_specs=[away] * 10,
        out_specs=[whole, whole],
        scratch_shapes=[
            held(2048, 1024),
            held(1024, 3072),
            held(1024, 1024),
            dma((3, N_IDS)),
            dma((3, N_IDS)),
            dma((3,)),
            dma((3, 5)),
            dma((3, 5)),
            dma((2, 5)),
            dma((2, 5)),
            held(OUT_ROWS, 128),
            held(IN_ROWS, 128),
            held(432, 256),
            held(144, 512),
            held(432, 256),
            held(144, 512),
            held(576, 256),
            held(144, 512),
            held(576, 256),
            held(144, 512),
            held(576, 256),
            held(144, 512),
            held(576, 256),
            held(144, 512),
            held(432, 256),
            held(144, 512),
            held(432, 256),
            held(144, 512),
            held(288, 2048),
            held(288, 2048, dtype=F32),
            held(288, 128, dtype=F32),
            held(288, 1024),
            held(288, 1024),
            held(288, 1024),
            held(288, 1024),
            held(288, 3072),
            held(288, 1024),
            held(288, 1024),
            held(288, 3072),
            held(288, 1024, dtype=F32),
            held(288, 2048, dtype=F32),
            held(12, 16, 384, dtype=F32),
            held(48, 640),
            held(2304, 144, dtype=F32),
            held(2, 144, 144, dtype=F32),
            held(16, 128, dtype=F32),
            held(288, 128, dtype=F32),
            held(1152, 512),
            held(288, 1024),
            held(1, 2048, dtype=F32),
            held(1, 1024, dtype=F32),
            held(16, 529, dtype=F32),
            held(12, 24, dtype=jnp.int32),
            held(1, 16, dtype=jnp.int32),
            dma((7,)),
            held(2, 288, 144, dtype=F32),
            held(2, 288, 144, dtype=F32),
            held(2, 288, 144),
            held(2, 288, 144),
        ],
        compiler_params=pltpu.CompilerParams(
            collective_id=0, has_side_effects=True, vmem_limit_bytes=60 << 20
        ),
        cost_estimate=pl.CostEstimate(
            flops=10_000_000_000, bytes_accessed=20_000_000, transcendentals=700_000
        ),
    )(
        fine.reshape(1152, 512),
        merge_gain.reshape(1, 2048),
        merge_w,
        attn_gain.reshape(1, 1024),
        qkv_w,
        proj_w,
        table,
        region,
        counts.reshape(1, 16),
        cot.reshape(288, 1024),
    )
    return out.reshape(12, 24, 1024), grad_fine.reshape(24, 48, 512)


def solution(mesh):
    grid = P("lat", "lon", None)
    rows = P("lat", None)
    return jax.shard_map(
        local,
        mesh=mesh,
        in_specs=(grid, P(), rows, P(), rows, rows, P(), P("lat", "lon"), P(), grid),
        out_specs=(grid, grid),
        check_vma=False,
    )
```
